512 devices in a mesh: terms: 8 (over x, core), sectors: 64 (over z, y).
Axes of the slice: x: 4, y: 4, z: 16, core: 2. Of those that a mesh axis runs over, the one named last changes fastest.
Arguments:
- wave: float32 [512, 64, 512], P('sectors'), may hold values from -45 to 45
- left_env: float32 [8, 512, 4096], P('terms', 'sectors'), may hold values from -3 to 3
- right_env: float32 [8, 512, 4096], P('terms', 'sectors'), may hold values from -4 to 4
- pair_target: int32 [512, 8], replicated, may hold values from 0 to 511, as said below
- block_dims: int32 [512], replicated, may hold values from 32 to 64
Outputs:
- image_two: float32 [512, 64, 512], P('sectors')
- projected: float32 [2, 2], replicated
The draws below stay inside these ranges and needn't reach their ends.
Inputs may be any that keep to these rules, and one draw needn't show every extreme that they name: `pair_target`: every right sector is named exactly 8 times. Counting sectors in runs of 8 (a run to an index of sectors), the blocks of one run of left sectors name exactly 1 right sectors of every run.
All inputs are finite; a program needn't handle non-finite values.
Results may differ from the reference program's by a relative error of at most 0.0003.
Values sent between devices are 32-bit elements; how exact they have to be, the bound alone decides.
A program may use at most 64 MiB of HBM per device.

```python
import math
import jax
import jax.numpy as jnp
from jax import lax

SEC_DEV = 8
PAIRS = 8
DB = 64
GROUPS = 8
NS = 512


def env_blocks(diagonal, jitter_vals):
    index_row = jnp.arange(DB)
    grade = 0.25 + 1.25 * index_row.astype(jnp.float32) / (DB - 1)
    identity = (index_row[:, None] == index_row[None, :]).astype(jnp.float32)
    full = diagonal * (identity * grade[None, :]) + jitter_vals / math.sqrt(DB)
    return full.reshape(GROUPS, NS, DB * DB)


def sector_growth(base):
    sector_ids = jnp.arange(NS, dtype=jnp.int32)
    local_pos = (sector_ids % SEC_DEV).astype(jnp.float32) / (SEC_DEV - 1)
    run_pos = (sector_ids // SEC_DEV).astype(jnp.float32) / (NS // SEC_DEV - 1)
    return (base ** local_pos * base ** run_pos)[:, None, None, None]


def decay_profile(key, lowest, highest):
    key_row, key_col = jax.random.split(key)
    row_rate = jax.random.uniform(key_row, (NS, 1, 1, 1), jnp.float32, lowest, highest)
    col_rate = jax.random.uniform(key_col, (NS, PAIRS, 1, 1), jnp.float32, lowest, highest)
    place = jnp.arange(DB).astype(jnp.float32) / DB
    return jnp.exp(-row_rate * place[:, None]) * jnp.exp(-col_rate * place[None, :])


def draw_wave(key, part):
    key = jax.random.fold_in(key, 5)
    key_vals, key_prof = jax.random.split(key)
    values = jnp.clip(jax.random.normal(key_vals, (NS, PAIRS, DB, DB), jnp.float32), -5.0, 5.0)
    growth = sector_growth(3.0)
    profile = decay_profile(key_prof, 2.5, 4.5)
    blocks = values * growth * profile
    return blocks.transpose(0, 2, 1, 3).reshape(NS, DB, PAIRS * DB)


def draw_left_env(key, part):
    key = jax.random.fold_in(key, 7)
    key_diag, key_jitter = jax.random.split(key)
    jitter_vals = jnp.clip(jax.random.normal(key_jitter, (GROUPS, NS, DB, DB), jnp.float32), -5.0, 5.0)
    diagonal = jax.random.uniform(key_diag, (GROUPS, NS, 1, 1), jnp.float32, 0.5, 1.5)
    return env_blocks(diagonal, jitter_vals) / math.sqrt(GROUPS)


def draw_right_env(key, part):
    key = jax.random.fold_in(key, 9)
    key_diag, key_jitter = jax.random.split(key)
    jitter_vals = jnp.clip(jax.random.normal(key_jitter, (GROUPS, NS, DB, DB), jnp.float32), -5.0, 5.0)
    diagonal = jax.random.uniform(key_diag, (GROUPS, NS, 1, 1), jnp.float32, 0.5, 1.5)
    return env_blocks(diagonal, jitter_vals)


def draw_pair_target(key, part):
    key = jax.random.fold_in(key, 17)
    key_one, key_two, key_three, key_four = jax.random.split(key, 4)
    devices = NS // SEC_DEV
    blocks = SEC_DEV * PAIRS
    outer_perm = jax.random.permutation(key_one, devices)
    inner_perm = jax.random.permutation(key_two, devices)
    offsets = jax.random.permutation(key_three, blocks) % devices
    sectors = jax.random.permutation(key_four, blocks) // PAIRS
    source_dev = jnp.arange(devices)[:, None]
    target_dev = inner_perm[(outer_perm[source_dev] + offsets[None, :]) % devices]
    return (target_dev * SEC_DEV + sectors[None, :]).reshape(NS, PAIRS).astype(jnp.int32)


def plant(values, rng, smallest, high):
    longest = values.shape.index(max(values.shape))
    spots = []
    for shift in (0, 1):
        where = [jax.random.randint(jax.random.fold_in(rng, axis), (), 0, length) for axis, length in enumerate(values.shape)]
        where[longest] = (where[longest] + shift) % values.shape[longest]
        spots.append(tuple(where))
    return values.at[spots[0]].set(smallest).at[spots[1]].set(high)


def setup_inputs(seed: int = 0) -> dict:
    streams_of = jax.random.split(jax.random.key(seed), 6)
    wave = draw_wave(jax.random.fold_in(streams_of[5], 71), 0)
    left_env = draw_left_env(jax.random.fold_in(streams_of[5], 71), 0)
    right_env = draw_right_env(jax.random.fold_in(streams_of[5], 71), 0)
    pair_target = draw_pair_target(jax.random.fold_in(streams_of[5], 71), 0)
    block_dims = plant(jax.random.randint(streams_of[4], (NS,), DB // 2, DB + 1), jax.random.fold_in(streams_of[4], 1), DB // 2, DB).astype(jnp.int32)
    return {"wave": wave, "left_env": left_env, "right_env": right_env, "pair_target": pair_target, "block_dims": block_dims}


def hamiltonian(vector, left_env, right_env, pair_target, valid_mask):

    def per_sector(sector_id):
        left_blocks = left_env[:, sector_id]
        right_blocks = jnp.take(right_env, pair_target[sector_id], axis=1)
        inner_prod = jnp.einsum('tab,jbc->tjac', left_blocks, vector[sector_id], precision=lax.Precision.HIGHEST)
        return jnp.einsum('tjac,tjbc->jab', inner_prod, right_blocks, precision=lax.Precision.HIGHEST)
    result = lax.map(per_sector, jnp.arange(NS, dtype=jnp.int32))
    return result * valid_mask

def reference(wave, left_env, right_env, pair_target, block_dims):
    wave_blocks = wave.reshape(NS, DB, PAIRS, DB).transpose(0, 2, 1, 3)
    left_blocks = left_env.reshape(GROUPS, NS, DB, DB)
    right_blocks = right_env.reshape(GROUPS, NS, DB, DB)
    positions = jnp.arange(DB, dtype=jnp.int32)
    right_dims = jnp.take(block_dims, pair_target, axis=0)
    rows_ok = positions[None, None, :, None] < block_dims[:, None, None, None]
    cols_ok = positions[None, None, None, :] < right_dims[:, :, None, None]
    valid_mask = (rows_ok & cols_ok).astype(jnp.float32)
    cell_total = jnp.float32(NS * PAIRS * DB * DB)
    first_vec = wave_blocks * valid_mask
    image_one = hamiltonian(first_vec, left_blocks, right_blocks, pair_target, valid_mask)
    norm_first = jnp.sum(first_vec * first_vec)
    cross_dot = jnp.sum(first_vec * image_one)
    energy = cross_dot / norm_first
    residual = image_one - energy * first_vec
    squared = jnp.sum(residual * residual)
    direction = residual / jnp.sqrt(squared / cell_total + 1e-06)
    image_two = hamiltonian(direction, left_blocks, right_blocks, pair_target, valid_mask)
    first_two = jnp.sum(first_vec * image_two)
    dir_one = jnp.sum(direction * image_one)
    dir_two = jnp.sum(direction * image_two)
    projected = jnp.stack([jnp.stack([cross_dot, first_two]), jnp.stack([dir_one, dir_two])]) / cell_total
    image_flat = image_two.transpose(0, 2, 1, 3).reshape(NS, DB, PAIRS * DB)
    return (image_flat, projected)
```

```python
import functools

import jax
import jax.numpy as jnp
from jax import lax
from jax.experimental import pallas as pl
from jax.experimental.pallas import tpu as pltpu
from jax.sharding import PartitionSpec as P

MESH = pl.DeviceIdType.MESH
DB = 64
LANES = 128
HALF = DB // 2
WIDE_Y = 4
TINY = 1e-30
NAMES = ("n", "c", "rr", "rf", "fg", "ri", "rg", "e")


def lane_low(rows):
    return lax.broadcasted_iota(jnp.int32, (rows, LANES), 1) < DB


def swap(x):
    return pltpu.roll(x, DB, 1)


def split(x):
    high = x.astype(jnp.bfloat16)
    low = (x - high.astype(jnp.float32)).astype(jnp.bfloat16)
    return high, low


def total(x):
    return jnp.sum(jnp.sum(x, axis=0, keepdims=True), axis=1, keepdims=True)


def recenter(stat, center):
    shift = stat["e"] - center
    return {
        "n": stat["n"],
        "c": stat["c"],
        "rr": stat["rr"] + 2.0 * shift * stat["rf"] + shift * shift * stat["n"],
        "rf": stat["rf"] + shift * stat["n"],
        "fg": stat["fg"] + shift * stat["c"],
        "ri": stat["ri"] + shift * stat["c"],
        "rg": stat["rg"] + shift * (stat["ri"] + stat["fg"]) + shift * shift * stat["c"],
    }


def quotient(cross, norm):
    return jnp.where(norm > TINY, cross / jnp.maximum(norm, TINY), 0.0)


def merge(stat, last):
    norm = jnp.sum(stat["n"], axis=0, keepdims=True)
    cross = jnp.sum(stat["c"], axis=0, keepdims=True)
    center = cross / norm if last else quotient(cross, norm)
    moved = recenter(stat, center)
    out = {name: jnp.sum(value, axis=0, keepdims=True) for name, value in moved.items()}
    out["e"] = center
    return out


def read_rows(buf):
    rows = buf[:, 0, :]
    return {name: rows[:, k : k + 1] for k, name in enumerate(NAMES)}


def row_of(stat):
    lane = lax.broadcasted_iota(jnp.int32, (1, LANES), 1)
    row = jnp.zeros((1, LANES), jnp.float32)
    for k, name in enumerate(NAMES):
        row = jnp.where(lane == k, stat[name], row)
    return row


def repack(src, dst):
    low = lane_low(src.shape[0])
    for u in range(HALF // 2):
        first = src[:, LANES * u : LANES * (u + 1)]
        second = src[:, LANES * (u + HALF // 2) : LANES * (u + HALF // 2 + 1)]
        dst[:, 2 * u, :] = jnp.where(low, first, swap(second))
        dst[:, 2 * u + 1, :] = jnp.where(low, swap(first), second)


def kernel(
    geo,
    cells,
    tab,
    dims,
    wave_hbm,
    left_ref,
    right_ref,
    out_ref,
    proj_ref,
    wave,
    zbuf,
    stage,
    rrecv,
    lall,
    lbf,
    wcat,
    rcat,
    ibuf,
    gbuf,
    stat_ref,
    red_a,
    red_b,
    fbuf,
    wave_sem,
    z_send,
    z_recv,
    p_send,
    p_recv,
    l_send,
    l_recv,
    a_send,
    a_recv,
    b_send,
    b_recv,
    f_send,
    f_recv,
):
    wide_x, wide_y, wide_z = geo
    terms = 2 * wide_x
    nblk = wide_z // 2
    half_z = wide_z // 2
    sec = left_ref.shape[0]
    chunks = z_send.shape[1]
    csec = sec // chunks
    plane = terms * wide_y

    my_t = lax.axis_index("terms")
    my_s = lax.axis_index("sectors")
    my_x = my_t // 2
    my_c = my_t % 2
    my_z = my_s // wide_y
    my_y = my_s % wide_y

    def dev(t, z, y):
        return {"terms": t, "sectors": z * wide_y + y}

    def plane_peer(i):
        other = lax.rem(my_t * wide_y + my_y + i, plane)
        return dev(other // wide_y, my_z, other % wide_y)

    def z_peer(i):
        return dev(my_t, lax.rem(my_z + i, wide_z), my_y)

    barrier = pltpu.get_barrier_semaphore()

    def greet_plane(i, carry):
        pl.semaphore_signal(barrier, inc=1, device_id=plane_peer(i), device_id_type=MESH)
        return carry

    def greet_z(i, carry):
        pl.semaphore_signal(barrier, inc=1, device_id=z_peer(i), device_id_type=MESH)
        return carry

    lax.fori_loop(1, wide_z, greet_z, 0)
    lax.fori_loop(1, plane, greet_plane, 0)
    wave_copy = pltpu.make_async_copy(wave_hbm, wave, wave_sem)
    wave_copy.start()
    repack(right_ref, zbuf.at[0])
    repack(left_ref, lall.at[my_t])
    pl.semaphore_wait(barrier, plane - 1 + wide_z - 1)

    def z_copy(src, dst, k, peer):
        part = pl.ds(k * csec, csec)
        return pltpu.make_async_remote_copy(
            src_ref=zbuf.at[src, part],
            dst_ref=zbuf.at[dst, part],
            send_sem=z_send.at[dst, k],
            recv_sem=z_recv.at[dst, k],
            device_id=peer,
            device_id_type=MESH,
        )

    up, down = z_peer(1), z_peer(wide_z - 1)

    def forward_up(d, k):
        z_copy(d, d + 1, k, up).start()

    def forward_down(d, k):
        z_copy(lax.rem(wide_z - d, wide_z), wide_z - 1 - d, k, down).start()

    sibling = dev(my_t + 1 - 2 * my_c, my_z, my_y)

    def l_copy(t, peer, k):
        return pltpu.make_async_remote_copy(
            src_ref=lall.at[t],
            dst_ref=lall.at[t],
            send_sem=l_send.at[k],
            recv_sem=l_recv.at[t],
            device_id=peer,
            device_id_type=MESH,
        )

    def x_term(i):
        return lax.rem(my_x + i, wide_x) * 2 + my_c

    for k in range(chunks):
        forward_up(0, k)
        forward_down(0, k)
    for i in range(1, wide_x):
        l_copy(my_t, dev(x_term(i), my_z, my_y), i - 1).start()
    l_copy(my_t, sibling, wide_x - 1).start()

    def owner(o, yp):
        t = 2 * lax.rem(my_y + yp + o, wide_x) + o // half_z
        return t, jnp.logical_and(t == my_t, yp == my_y)

    def remote_piece(o, yp):
        t, _ = owner(o, yp)
        return pltpu.make_async_remote_copy(
            src_ref=stage.at[o, yp],
            dst_ref=rrecv.at[lax.rem(o, half_z), my_t],
            send_sem=p_send.at[o, yp],
            recv_sem=p_recv.at[lax.rem(o, half_z)],
            device_id=dev(t, my_z, yp),
            device_id_type=MESH,
        )

    def local_piece(o, yp):
        b = lax.rem(o, half_z)
        return pltpu.make_async_copy(stage.at[o, yp], rrecv.at[b, my_t], p_recv.at[b])

    def hand_out(o):
        def one(yp, carry):
            wanted = jnp.full((HALF, LANES), tab[o * wide_y + yp], jnp.int32)
            got = zbuf[o, 0]
            for k in range(1, sec):
                got = jnp.where(wanted == k, zbuf[o, k], got)
            stage[o, yp] = got
            _, mine = owner(o, yp)

            @pl.when(mine)
            def _():
                local_piece(o, yp).start()

            @pl.when(jnp.logical_not(mine))
            def _():
                remote_piece(o, yp).start()

            return carry

        lax.fori_loop(0, wide_y, one, 0)

    def arrive(o, k):
        z_copy(o, o, k, up).wait_recv()

    def z_step(d):
        def part(k, carry):
            arrive(d, k)
            forward_up(d, k)
            arrive(wide_z - d, k)
            forward_down(d, k)
            return carry

        lax.fori_loop(0, chunks, part, 0)
        hand_out(d)
        hand_out(wide_z - d)

    def z_step_before_last(d):
        for k in range(chunks):
            arrive(d, k)
            if k < chunks // 2:
                forward_up(d, k)
            arrive(wide_z - d, k)
            if k >= chunks // 2:
                forward_down(d, k)
        hand_out(d)
        hand_out(wide_z - d)

    def z_step_last(d):
        for k in range(chunks):
            arrive(d, k)
        hand_out(d)

    low64 = lane_low(DB)
    low32 = lane_low(HALF)
    slot_at = wide_z * wide_y
    sector_at = slot_at + cells
    column_at = sector_at + nblk
    odd_at = column_at + nblk
    target_at = odd_at + nblk
    pairs = cells // sec

    def apply(vec, q):
        vh, vl = split(vec)
        rhs = jnp.concatenate([vh, vh, vl, vl], axis=0)
        for u in range(terms // 2):
            lhs = lbf[q, pl.ds(u * LANES, LANES), :]
            both = jnp.dot(
                jnp.concatenate([lhs, lhs], axis=1), rhs, preferred_element_type=jnp.float32
            )
            high, low = split(jnp.where(low64, both[:DB], both[DB:]))
            wcat[:DB, u * LANES : (u + 1) * LANES] = high
            wcat[DB:, u * LANES : (u + 1) * LANES] = low
        out = lax.dot_general(
            wcat[...], rcat[...], (((1,), (1,)), ((), ())), preferred_element_type=jnp.float32
        )
        out = out[:DB] + out[DB:]
        return out + swap(out)

    def pack(x):
        return jnp.where(low32, x[:HALF], x[HALF:])

    def work(i):
        b = jnp.where(my_c == 0, i, nblk - 1 - i)
        pltpu.make_async_copy(rrecv.at[b], rrecv.at[b], p_recv.at[b]).wait()
        for u in range(terms // 2):
            first, second = rrecv[b, 2 * u], rrecv[b, 2 * u + 1]
            top = jnp.where(low32, first, swap(second))
            bottom = jnp.where(low32, swap(first), second)
            high, low = split(jnp.concatenate([top, bottom], axis=0))
            rcat[:DB, u * LANES : (u + 1) * LANES] = high
            rcat[DB:, u * LANES : (u + 1) * LANES] = low
        q = tab[sector_at + b]
        column = jnp.full((DB, LANES), tab[column_at + b], jnp.int32)
        odd = jnp.full((DB, LANES), tab[odd_at + b], jnp.int32)
        raw = wave[q, :, 0:LANES]
        for u in range(1, pairs // 2):
            raw = jnp.where(column == u, wave[q, :, u * LANES : (u + 1) * LANES], raw)
        lane = lax.broadcasted_iota(jnp.int32, (DB, LANES), 1)
        row = lax.broadcasted_iota(jnp.int32, (DB, LANES), 0)
        raw = jnp.where(lane // DB == odd, raw, swap(raw))
        used = jnp.logical_and(
            row < dims[my_s * sec + q], lax.rem(lane, DB) < dims[tab[target_at + b]]
        )
        first = jnp.where(used, raw, 0.0)
        image = jnp.where(used, apply(first, q), 0.0)
        norm = 0.5 * total(first * first)
        cross = 0.5 * total(first * image)
        energy = quotient(cross, norm)
        rest = image - energy * first
        second = jnp.where(used, apply(rest, q), 0.0)
        ibuf[b] = pack(image)
        gbuf[b] = pack(second)
        values = (
            norm,
            cross,
            0.5 * total(rest * rest),
            0.5 * total(rest * first),
            0.5 * total(first * second),
            0.5 * total(rest * image),
            0.5 * total(rest * second),
            energy,
        )
        sub = lax.broadcasted_iota(jnp.int32, (8, LANES), 0)
        tile = jnp.zeros((8, LANES), jnp.float32)
        for k, value in enumerate(values):
            tile = jnp.where(sub == k, value, tile)
        stat_ref[b] = tile

    def unpack_left():
        def one(t, carry):
            for q in range(sec):
                x = lall[t, q]
                high, low = split(x)
                high, low = high.astype(jnp.float32), low.astype(jnp.float32)
                top = jnp.where(low32, high, swap(low))
                bottom = jnp.where(low32, swap(high), low)
                both = jnp.concatenate([top, bottom], axis=0).astype(jnp.bfloat16)
                lbf[q, pl.ds(pl.multiple_of(t * DB, DB), DB), :] = both
            return carry

        lax.fori_loop(0, terms, one, 0)

    early = min(3, half_z - 1)
    hand_out(0)
    for i in range(1, wide_x):
        t = x_term(i)
        l_copy(t, sibling, 0).wait_recv()
        l_copy(t, sibling, wide_x - 1 + i).start()
    lax.fori_loop(1, early, lambda d, c: (z_step(d), c)[1], 0)
    for i in range(wide_x):
        l_copy(lax.rem(my_x + i, wide_x) * 2 + 1 - my_c, sibling, 0).wait_recv()
    unpack_left()
    wave_copy.wait()

    def mixed(d, carry):
        z_step(d)
        work(d - early)
        return carry

    lax.fori_loop(early, half_z - 1, mixed, 0)
    z_step_before_last(half_z - 1)
    work(half_z - 1 - early)
    z_step_last(half_z)

    def rest_of_work(i, carry):
        work(i)
        return carry

    lax.fori_loop(half_z - early, nblk, rest_of_work, 0)

    stat = {name: stat_ref[:, k, :] for k, name in enumerate(NAMES)}
    mine = my_t * wide_y + my_y
    red_a[mine] = row_of(merge(stat, False))

    def a_copy(i):
        return pltpu.make_async_remote_copy(
            src_ref=red_a.at[mine],
            dst_ref=red_a.at[mine],
            send_sem=a_send.at[i],
            recv_sem=a_recv,
            device_id=plane_peer(i),
            device_id_type=MESH,
        )

    def b_copy(i):
        return pltpu.make_async_remote_copy(
            src_ref=red_b.at[my_z],
            dst_ref=red_b.at[my_z],
            send_sem=b_send.at[i],
            recv_sem=b_recv,
            device_id=z_peer(i),
            device_id_type=MESH,
        )

    lax.fori_loop(1, plane, lambda i, c: (a_copy(i).start(), c)[1], 0)
    pltpu.make_async_copy(
        red_a.at[pl.ds(0, plane - 1)], red_a.at[pl.ds(0, plane - 1)], a_recv
    ).wait()
    red_b[my_z] = row_of(merge(read_rows(red_a), False))
    lax.fori_loop(1, wide_z, lambda i, c: (b_copy(i).start(), c)[1], 0)
    pltpu.make_async_copy(
        red_b.at[pl.ds(0, wide_z - 1)], red_b.at[pl.ds(0, wide_z - 1)], b_recv
    ).wait()
    final = merge(read_rows(red_b), True)
    cell_total = float(plane * wide_z * nblk * DB * DB)
    squared = jnp.maximum(final["rr"], 0.0)
    scale = 1.0 / jnp.sqrt(squared / cell_total + 1e-06)
    sub2 = lax.broadcasted_iota(jnp.int32, (2, 2), 0)
    lane2 = lax.broadcasted_iota(jnp.int32, (2, 2), 1)
    proj_ref[...] = (
        jnp.where(
            sub2 == 0,
            jnp.where(lane2 == 0, final["c"], final["fg"] * scale),
            jnp.where(lane2 == 0, final["ri"] * scale, final["rg"] * scale * scale),
        )
        / cell_total
    )

    center = final["e"]
    for b in range(nblk):
        shift = stat_ref[b, 7:8, :] - center
        fbuf[my_t * nblk + b] = (gbuf[b] + shift * ibuf[b]) * scale

    def f_copy(t, peer, k):
        return pltpu.make_async_remote_copy(
            src_ref=fbuf.at[pl.ds(t * nblk, nblk)],
            dst_ref=fbuf.at[pl.ds(t * nblk, nblk)],
            send_sem=f_send.at[k],
            recv_sem=f_recv.at[t],
            device_id=peer,
            device_id_type=MESH,
        )

    for i in range(1, wide_x):
        f_copy(my_t, dev(x_term(i), my_z, my_y), i - 1).start()
    f_copy(my_t, sibling, wide_x - 1).start()
    for i in range(1, wide_x):
        t = x_term(i)
        f_copy(t, sibling, 0).wait_recv()
        f_copy(t, sibling, wide_x - 1 + i).start()
    for i in range(wide_x):
        f_copy(lax.rem(my_x + i, wide_x) * 2 + 1 - my_c, sibling, 0).wait_recv()

    def place(q, carry):
        for u in range(pairs // 2):
            first_at = tab[slot_at + q * pairs + 2 * u]
            second_at = tab[slot_at + q * pairs + 2 * u + 1]
            first = fbuf[first_at]
            second = fbuf[second_at]
            out_ref[q, 0:HALF, u * LANES : (u + 1) * LANES] = jnp.where(
                low32, first, swap(second)
            )
            out_ref[q, HALF:DB, u * LANES : (u + 1) * LANES] = jnp.where(
                low32, swap(first), second
            )
        return carry

    lax.fori_loop(0, sec, place, 0)

    def z_done(d, carry):
        for k in range(chunks):
            z_copy(0, d + 1, k, up).wait_send()
            z_copy(0, wide_z - 1 - d, k, down).wait_send()
        return carry

    lax.fori_loop(0, half_z - 1, z_done, 0)
    for k in range(chunks):
        z_copy(0, half_z, k, up).wait_send()

    def p_done(n, carry):
        o, yp = n // wide_y, lax.rem(n, wide_y)
        _, mine = owner(o, yp)

        @pl.when(jnp.logical_not(mine))
        def _():
            remote_piece(o, yp).wait_send()

        return carry

    lax.fori_loop(0, wide_z * wide_y, p_done, 0)
    for i in range(2 * wide_x - 1):
        l_copy(my_t, sibling, i).wait_send()
        f_copy(my_t, sibling, i).wait_send()
    lax.fori_loop(1, plane, lambda i, c: (a_copy(i).wait_send(), c)[1], 0)
    lax.fori_loop(1, wide_z, lambda i, c: (b_copy(i).wait_send(), c)[1], 0)


def tables(geo, sec, pairs, pair_target):
    wide_x, wide_y, wide_z = geo
    nblk = wide_z // 2
    half_z = wide_z // 2
    my_t = lax.axis_index("terms")
    my_s = lax.axis_index("sectors")
    my_z, my_y = my_s // wide_y, my_s % wide_y
    cells = sec * pairs
    plane = lax.dynamic_slice_in_dim(pair_target, my_z * wide_y * sec, wide_y * sec, 0)
    plane = plane.reshape(wide_y, cells)
    offsets = jnp.arange(wide_z, dtype=jnp.int32)
    run = jnp.remainder(my_z - offsets, wide_z) * wide_y + my_y
    hit = (plane // sec)[None, :, :] == run[:, None, None]
    wanted = jnp.sum(jnp.where(hit, (plane % sec)[None, :, :], 0), axis=2).reshape(-1)
    own = lax.dynamic_slice_in_dim(pair_target, my_s * sec, sec, 0).reshape(cells)
    own_run = own // sec
    offset = jnp.remainder(my_z - own_run // wide_y, wide_z)
    holder = 2 * ((own_run % wide_y + my_y + offset) % wide_x) + offset // half_z
    slot = holder * nblk + offset % half_z
    chosen = slot[None, :] == (my_t * nblk + jnp.arange(nblk, dtype=jnp.int32))[:, None]
    cell = jnp.sum(jnp.where(chosen, jnp.arange(cells, dtype=jnp.int32)[None, :], 0), axis=1)
    target = jnp.sum(jnp.where(chosen, own[None, :], 0), axis=1)
    column = cell % pairs
    return jnp.concatenate([wanted, slot, cell // pairs, column // 2, column % 2, target])


def per_device(wide_y, wave, left_env, right_env, pair_target, block_dims):
    terms = lax.axis_size("terms")
    devices = lax.axis_size("sectors")
    geo = (terms // 2, wide_y, devices // wide_y)
    sec = wave.shape[0]
    pairs = wave.shape[2] // DB
    cells = sec * pairs
    nblk = geo[2] // 2
    plane = terms * wide_y
    chunks = 2
    tab = tables(geo, sec, pairs, pair_target)
    f32, bf16 = jnp.float32, jnp.bfloat16
    dma = pltpu.SemaphoreType.DMA
    vmem = pl.BlockSpec(memory_space=pltpu.VMEM)
    smem = pl.BlockSpec(memory_space=pltpu.SMEM)
    return pl.pallas_call(
        functools.partial(kernel, geo, cells),
        out_shape=(
            jax.ShapeDtypeStruct(wave.shape, f32),
            jax.ShapeDtypeStruct((2, 2), f32),
        ),
        in_specs=[smem, smem, pl.BlockSpec(memory_space=pl.ANY), vmem, vmem],
        out_specs=(vmem, vmem),
        scratch_shapes=[
            pltpu.VMEM(wave.shape, f32),
            pltpu.VMEM((geo[2], sec, HALF, LANES), f32),
            pltpu.VMEM((geo[2], wide_y, HALF, LANES), f32),
            pltpu.VMEM((nblk, terms, HALF, LANES), f32),
            pltpu.VMEM((terms, sec, HALF, LANES), f32),
            pltpu.VMEM((sec, terms * DB, LANES), bf16),
            pltpu.VMEM((LANES, terms * DB), bf16),
            pltpu.VMEM((LANES, terms * DB), bf16),
            pltpu.VMEM((nblk, HALF, LANES), f32),
            pltpu.VMEM((nblk, HALF, LANES), f32),
            pltpu.VMEM((nblk, 8, LANES), f32),
            pltpu.VMEM((plane, 1, LANES), f32),
            pltpu.VMEM((geo[2], 1, LANES), f32),
            pltpu.VMEM((terms * nblk, HALF, LANES), f32),
            dma,
            dma((geo[2], chunks)),
            dma((geo[2], chunks)),
            dma((geo[2], wide_y)),
            dma((nblk,)),
            dma((2 * geo[0] - 1,)),
            dma((terms,)),
            dma((plane,)),
            dma,
            dma((geo[2],)),
            dma,
            dma((2 * geo[0] - 1,)),
            dma((terms,)),
        ],
        compiler_params=pltpu.CompilerParams(
            collective_id=0, has_side_effects=True, vmem_limit_bytes=32 * 1024 * 1024
        ),
    )(
        tab,
        block_dims,
        wave,
        left_env.reshape(sec, DB * DB),
        right_env.reshape(sec, DB * DB),
    )


def solution(mesh, wide_y=WIDE_Y):
    in_specs = (
        P("sectors", None, None),
        P("terms", "sectors", None),
        P("terms", "sectors", None),
        P(),
        P(),
    )
    out_specs = (P("sectors", None, None), P())
    return jax.shard_map(
        functools.partial(per_device, wide_y),
        mesh=mesh,
        in_specs=in_specs,
        out_specs=out_specs,
        check_vma=False,
    )
```

```python
import functools

import jax
import jax.numpy as jnp
from jax import lax
from jax.experimental import pallas as pl
from jax.experimental.pallas import tpu as pltpu
from jax.sharding import PartitionSpec as P

MESH = pl.DeviceIdType.MESH
DB = 64
LANES = 128
HALF = DB // 2
WIDE_Y = 4
STRIDE = 2
TINY = 1e-30
NAMES = ("n", "c", "rr", "rf", "fg", "ri", "rg", "e")


def lane_low(rows):
    return lax.broadcasted_iota(jnp.int32, (rows, LANES), 1) < DB


def swap(x):
    return pltpu.roll(x, DB, 1)


def split(x):
    high = x.astype(jnp.bfloat16)
    low = (x - high.astype(jnp.float32)).astype(jnp.bfloat16)
    return high, low


def total(x):
    return jnp.sum(jnp.sum(x, axis=0, keepdims=True), axis=1, keepdims=True)


def recenter(stat, center):
    shift = stat["e"] - center
    return {
        "n": stat["n"],
        "c": stat["c"],
        "rr": stat["rr"] + 2.0 * shift * stat["rf"] + shift * shift * stat["n"],
        "rf": stat["rf"] + shift * stat["n"],
        "fg": stat["fg"] + shift * stat["c"],
        "ri": stat["ri"] + shift * stat["c"],
        "rg": stat["rg"] + shift * (stat["ri"] + stat["fg"]) + shift * shift * stat["c"],
    }


def quotient(cross, norm):
    return jnp.where(norm > TINY, cross / jnp.maximum(norm, TINY), 0.0)


def merge(stat, last):
    norm = jnp.sum(stat["n"], axis=0, keepdims=True)
    cross = jnp.sum(stat["c"], axis=0, keepdims=True)
    center = cross / norm if last else quotient(cross, norm)
    moved = recenter(stat, center)
    out = {name: jnp.sum(value, axis=0, keepdims=True) for name, value in moved.items()}
    out["e"] = center
    return out


def read_rows(buf):
    rows = buf[:, 0, :]
    return {name: rows[:, k : k + 1] for k, name in enumerate(NAMES)}


def row_of(stat):
    lane = lax.broadcasted_iota(jnp.int32, (1, LANES), 1)
    row = jnp.zeros((1, LANES), jnp.float32)
    for k, name in enumerate(NAMES):
        row = jnp.where(lane == k, stat[name], row)
    return row


def repack(src, dst):
    low = lane_low(src.shape[0])
    for u in range(HALF // 2):
        first = src[:, LANES * u : LANES * (u + 1)]
        second = src[:, LANES * (u + HALF // 2) : LANES * (u + HALF // 2 + 1)]
        dst[:, 2 * u, :] = jnp.where(low, first, swap(second))
        dst[:, 2 * u + 1, :] = jnp.where(low, swap(first), second)


def kernel(
    geo,
    cells,
    tab,
    dims,
    wave_hbm,
    left_ref,
    right_ref,
    out_ref,
    proj_ref,
    wave,
    zbuf,
    stage,
    rrecv,
    lall,
    lbf,
    wcat,
    rcat,
    gbuf,
    red_a,
    red_b,
    wave_sem,
    z_send,
    z_recv,
    p_send,
    p_recv,
    l_send,
    l_recv,
    a_send,
    a_recv,
    b_send,
    b_recv,
    g_send,
    g_pass,
    g_recv,
    plane_sem,
    space_sem,
):
    wide_x, wide_y, wide_z = geo
    terms = 2 * wide_x
    nblk = wide_z // 2
    half_z = wide_z // 2
    sec = left_ref.shape[0]
    chunks = z_send.shape[1]
    csec = sec // chunks
    plane = terms * wide_y

    my_t = lax.axis_index("terms")
    my_s = lax.axis_index("sectors")
    my_x = my_t // 2
    my_c = my_t % 2
    my_z = my_s // wide_y
    my_y = my_s % wide_y

    def dev(t, z, y):
        return {"terms": t, "sectors": z * wide_y + y}

    def plane_peer(i):
        other = lax.rem(my_t * wide_y + my_y + i, plane)
        return dev(other // wide_y, my_z, other % wide_y)

    def z_peer(i):
        return dev(my_t, lax.rem(my_z + i, wide_z), my_y)

    def y_peer(i):
        return dev(my_t, my_z, lax.rem(my_y + i, wide_y))

    def term_peer(i):
        return dev(lax.rem(my_t + i, terms), my_z, my_y)

    barrier = pltpu.get_barrier_semaphore()
    near = sorted({1, STRIDE, wide_z - STRIDE, wide_z - 1})

    def tell(sem, peers):
        for peer in peers:
            pl.semaphore_signal(sem, inc=1, device_id=peer, device_id_type=MESH)

    z_near = [z_peer(i) for i in near]
    y_near = [y_peer(i) for i in range(1, wide_y)]
    tell(barrier, z_near + y_near + [term_peer(i) for i in range(1, terms)])
    wave_copy = pltpu.make_async_copy(wave_hbm, wave, wave_sem)
    wave_copy.start()
    repack(right_ref, zbuf.at[0])
    repack(left_ref, lall.at[my_t])
    pl.semaphore_wait(barrier, len(near) + wide_y - 1 + terms - 1)

    def z_copy(src, dst, k, peer):
        part = pl.ds(k * csec, csec)
        return pltpu.make_async_remote_copy(
            src_ref=zbuf.at[src, part],
            dst_ref=zbuf.at[dst, part],
            send_sem=z_send.at[dst, k],
            recv_sem=z_recv.at[dst, k],
            device_id=peer,
            device_id_type=MESH,
        )

    up, down = z_peer(STRIDE), z_peer(wide_z - STRIDE)

    def forward_up(o, k):
        z_copy(o, o + STRIDE, k, up).start()

    def forward_down(o, k):
        z_copy(o, (o + wide_z - STRIDE) % wide_z, k, down).start()

    sibling = dev(my_t + 1 - 2 * my_c, my_z, my_y)

    def l_copy(t, peer, k):
        return pltpu.make_async_remote_copy(
            src_ref=lall.at[t],
            dst_ref=lall.at[t],
            send_sem=l_send.at[k],
            recv_sem=l_recv.at[t],
            device_id=peer,
            device_id_type=MESH,
        )

    def x_term(i):
        return lax.rem(my_x + i, wide_x) * 2 + my_c

    for k in range(chunks):
        forward_up(0, k)
        forward_down(0, k)
    for i in range(1, wide_x):
        l_copy(my_t, dev(x_term(i), my_z, my_y), i - 1).start()
    l_copy(my_t, sibling, wide_x - 1).start()

    tell(plane_sem, y_near)
    pl.semaphore_wait(plane_sem, wide_y - 1)
    tell(space_sem, z_near)
    pl.semaphore_wait(space_sem, len(near))

    def owner(far, step, yp):
        t = 2 * lax.rem(my_y + yp + far, wide_x) + far // half_z
        if step != 0:
            return t, jnp.bool_(False)
        return t, jnp.logical_and(t == my_t, yp == my_y)

    def remote_piece(far, step, yp):
        t, _ = owner(far, step, yp)
        return pltpu.make_async_remote_copy(
            src_ref=stage.at[far, yp],
            dst_ref=rrecv.at[far % half_z, my_t],
            send_sem=p_send.at[far, yp],
            recv_sem=p_recv.at[far % half_z],
            device_id=dev(t, lax.rem(my_z + (wide_z + step), wide_z), yp),
            device_id_type=MESH,
        )

    def local_piece(far, yp):
        b = far % half_z
        return pltpu.make_async_copy(stage.at[far, yp], rrecv.at[b, my_t], p_recv.at[b])

    def hand_out(o, step, first, last):
        far = (o + step) % wide_z

        def one(yp, carry):
            wanted = jnp.full((HALF, LANES), tab[far * wide_y + yp], jnp.int32)
            got = zbuf[o, 0]
            for k in range(1, sec):
                got = jnp.where(wanted == k, zbuf[o, k], got)
            stage[far, yp] = got
            if step != 0:
                remote_piece(far, step, yp).start()
                return carry
            _, mine = owner(far, step, yp)

            @pl.when(mine)
            def _():
                local_piece(far, yp).start()

            @pl.when(jnp.logical_not(mine))
            def _():
                remote_piece(far, step, yp).start()

            return carry

        lax.fori_loop(first, last, one, 0)

    def sent(o, step, first, last):
        far = (o + step) % wide_z

        def one(yp, carry):
            if step != 0:
                remote_piece(far, step, yp).wait_send()
                return carry
            _, mine = owner(far, step, yp)

            @pl.when(jnp.logical_not(mine))
            def _():
                remote_piece(far, step, yp).wait_send()

            return carry

        lax.fori_loop(first, last, one, 0)

    plan = piece_plan(geo)

    def arrive(o, k):
        z_copy(o, o, k, up).wait_recv()

    def level(n):
        last = n == len(plan) - 1
        for k in range(chunks):
            arrive(STRIDE * n, k)
            if not last:
                forward_up(STRIDE * n, k)
            arrive(wide_z - STRIDE * n, k)
            if not last:
                forward_down(wide_z - STRIDE * n, k)
        for one in plan[n]:
            hand_out(*one)

    low64 = lane_low(DB)
    low32 = lane_low(HALF)
    slot_at = wide_z * wide_y
    sector_at = slot_at + cells
    column_at = sector_at + nblk
    odd_at = column_at + nblk
    target_at = odd_at + nblk
    pairs = cells // sec

    def apply(vec, q):
        vh, vl = split(vec)
        rhs = jnp.concatenate([vh, vh, vl, vl], axis=0)
        for u in range(terms // 2):
            lhs = lbf[q, pl.ds(u * LANES, LANES), :]
            both = jnp.dot(
                jnp.concatenate([lhs, lhs], axis=1), rhs, preferred_element_type=jnp.float32
            )
            high, low = split(jnp.where(low64, both[:DB], both[DB:]))
            wcat[:DB, u * LANES : (u + 1) * LANES] = high
            wcat[DB:, u * LANES : (u + 1) * LANES] = low
        out = lax.dot_general(
            wcat[...], rcat[...], (((1,), (1,)), ((), ())), preferred_element_type=jnp.float32
        )
        out = out[:DB] + out[DB:]
        return out + swap(out)

    def pack(x):
        return jnp.where(low32, x[:HALF], x[HALF:])

    def work(i):
        b = jnp.where(my_c == 0, i, nblk - 1 - i)
        pltpu.make_async_copy(rrecv.at[b], rrecv.at[b], p_recv.at[b]).wait()
        for u in range(terms // 2):
            first, second = rrecv[b, 2 * u], rrecv[b, 2 * u + 1]
            top = jnp.where(low32, first, swap(second))
            bottom = jnp.where(low32, swap(first), second)
            high, low = split(jnp.concatenate([top, bottom], axis=0))
            rcat[:DB, u * LANES : (u + 1) * LANES] = high
            rcat[DB:, u * LANES : (u + 1) * LANES] = low
        q = tab[sector_at + b]
        column = jnp.full((DB, LANES), tab[column_at + b], jnp.int32)
        odd = jnp.full((DB, LANES), tab[odd_at + b], jnp.int32)
        raw = wave[q, :, 0:LANES]
        for u in range(1, pairs // 2):
            raw = jnp.where(column == u, wave[q, :, u * LANES : (u + 1) * LANES], raw)
        lane = lax.broadcasted_iota(jnp.int32, (DB, LANES), 1)
        row = lax.broadcasted_iota(jnp.int32, (DB, LANES), 0)
        raw = jnp.where(lane // DB == odd, raw, swap(raw))
        used = jnp.logical_and(
            row < dims[my_s * sec + q], lax.rem(lane, DB) < dims[tab[target_at + b]]
        )
        first = jnp.where(used, raw, 0.0)
        image = jnp.where(used, apply(first, q), 0.0)
        norm = 0.5 * total(first * first)
        cross = 0.5 * total(first * image)
        energy = quotient(cross, norm)
        rest = image - energy * first
        second = jnp.where(used, apply(rest, q), 0.0)
        gbuf[my_t, b, :HALF] = pack(second)
        gbuf[my_t, b, HALF:DB] = pack(image)
        values = (
            norm,
            cross,
            0.5 * total(rest * rest),
            0.5 * total(rest * first),
            0.5 * total(first * second),
            0.5 * total(rest * image),
            0.5 * total(rest * second),
            energy,
        )
        sub = lax.broadcasted_iota(jnp.int32, (8, LANES), 0)
        tile = jnp.zeros((8, LANES), jnp.float32)
        for k, value in enumerate(values):
            tile = jnp.where(sub == k, value, tile)
        gbuf[my_t, b, DB:] = tile
        for i in range(1, wide_x):
            g_block(b, i - 1, dev(x_term(i), my_z, my_y)).start()
        g_block(b, wide_x - 1, sibling).start()

    def g_block(b, k, peer):
        return pltpu.make_async_remote_copy(
            src_ref=gbuf.at[my_t, b],
            dst_ref=gbuf.at[my_t, b],
            send_sem=g_send.at[b, k],
            recv_sem=g_recv.at[my_t],
            device_id=peer,
            device_id_type=MESH,
        )

    def g_copy(t, k, peer):
        return pltpu.make_async_remote_copy(
            src_ref=gbuf.at[t],
            dst_ref=gbuf.at[t],
            send_sem=g_pass.at[k],
            recv_sem=g_recv.at[t],
            device_id=peer,
            device_id_type=MESH,
        )

    def unpack_left():
        def one(t, carry):
            for q in range(sec):
                x = lall[t, q]
                high, low = split(x)
                high, low = high.astype(jnp.float32), low.astype(jnp.float32)
                top = jnp.where(low32, high, swap(low))
                bottom = jnp.where(low32, swap(high), low)
                both = jnp.concatenate([top, bottom], axis=0).astype(jnp.bfloat16)
                lbf[q, pl.ds(pl.multiple_of(t * DB, DB), DB), :] = both
            return carry

        lax.fori_loop(0, terms, one, 0)

    for one in plan[0]:
        hand_out(*one)
    for i in range(1, wide_x):
        t = x_term(i)
        l_copy(t, sibling, 0).wait_recv()
        l_copy(t, sibling, wide_x - 1 + i).start()
    done = 0
    for n in range(1, len(plan)):
        level(n)
        if n == 1:
            for i in range(wide_x):
                l_copy(lax.rem(my_x + i, wide_x) * 2 + 1 - my_c, sibling, 0).wait_recv()
            unpack_left()
            wave_copy.wait()
        until = nblk if n == len(plan) - 1 else (1 if n == 1 else STRIDE * n)
        lax.fori_loop(done, until, lambda i, c: (work(i), c)[1], 0)
        done = until

    stat = {name: gbuf[my_t, :, DB + k, :] for k, name in enumerate(NAMES)}
    mine = my_t * wide_y + my_y
    red_a[mine] = row_of(merge(stat, False))

    def a_copy(i):
        return pltpu.make_async_remote_copy(
            src_ref=red_a.at[mine],
            dst_ref=red_a.at[mine],
            send_sem=a_send.at[i],
            recv_sem=a_recv,
            device_id=plane_peer(i),
            device_id_type=MESH,
        )

    def b_copy(i):
        return pltpu.make_async_remote_copy(
            src_ref=red_b.at[my_z],
            dst_ref=red_b.at[my_z],
            send_sem=b_send.at[i],
            recv_sem=b_recv,
            device_id=z_peer(i),
            device_id_type=MESH,
        )

    lax.fori_loop(1, plane, lambda i, c: (a_copy(i).start(), c)[1], 0)
    for i in range(1, wide_x):
        t = x_term(i)
        g_copy(t, i - 1, sibling).wait_recv()
        g_copy(t, i - 1, sibling).start()
    pltpu.make_async_copy(
        red_a.at[pl.ds(0, plane - 1)], red_a.at[pl.ds(0, plane - 1)], a_recv
    ).wait()
    red_b[my_z] = row_of(merge(read_rows(red_a), False))
    lax.fori_loop(1, wide_z, lambda i, c: (b_copy(i).start(), c)[1], 0)
    for i in range(wide_x):
        g_copy(lax.rem(my_x + i, wide_x) * 2 + 1 - my_c, 0, sibling).wait_recv()
    pltpu.make_async_copy(
        red_b.at[pl.ds(0, wide_z - 1)], red_b.at[pl.ds(0, wide_z - 1)], b_recv
    ).wait()
    final = merge(read_rows(red_b), True)
    cell_total = float(plane * wide_z * nblk * DB * DB)
    squared = jnp.maximum(final["rr"], 0.0)
    scale = 1.0 / jnp.sqrt(squared / cell_total + 1e-06)
    sub2 = lax.broadcasted_iota(jnp.int32, (2, 2), 0)
    lane2 = lax.broadcasted_iota(jnp.int32, (2, 2), 1)
    proj_ref[...] = (
        jnp.where(
            sub2 == 0,
            jnp.where(lane2 == 0, final["c"], final["fg"] * scale),
            jnp.where(lane2 == 0, final["ri"] * scale, final["rg"] * scale * scale),
        )
        / cell_total
    )

    center = final["e"]

    def block(at):
        t, b = at // nblk, lax.rem(at, nblk)
        shift = gbuf[t, b, DB + 7 : DB + 8, :] - center
        return (gbuf[t, b, :HALF] + shift * gbuf[t, b, HALF:DB]) * scale

    def place(q, carry):
        for u in range(pairs // 2):
            first = block(tab[slot_at + q * pairs + 2 * u])
            second = block(tab[slot_at + q * pairs + 2 * u + 1])
            out_ref[q, 0:HALF, u * LANES : (u + 1) * LANES] = jnp.where(
                low32, first, swap(second)
            )
            out_ref[q, HALF:DB, u * LANES : (u + 1) * LANES] = jnp.where(
                low32, swap(first), second
            )
        return carry

    lax.fori_loop(0, sec, place, 0)

    for n in range(len(plan) - 1):
        for k in range(chunks):
            z_copy(0, STRIDE * (n + 1), k, up).wait_send()
            z_copy(0, wide_z - STRIDE * (n + 1), k, down).wait_send()
    for pieces in plan:
        for one in pieces:
            sent(*one)
    for i in range(2 * wide_x - 1):
        l_copy(my_t, sibling, i).wait_send()

    def g_done(b, carry):
        for k in range(wide_x):
            g_block(b, k, sibling).wait_send()
        return carry

    lax.fori_loop(0, nblk, g_done, 0)
    for i in range(wide_x - 1):
        g_copy(my_t, i, sibling).wait_send()
    lax.fori_loop(1, plane, lambda i, c: (a_copy(i).wait_send(), c)[1], 0)
    lax.fori_loop(1, wide_z, lambda i, c: (b_copy(i).wait_send(), c)[1], 0)


def piece_plan(geo):
    _, wide_y, wide_z = geo
    levels = wide_z // (2 * STRIDE)
    plan = []
    for n in range(levels):
        o = STRIDE * n
        pieces = []
        for step in range(STRIDE):
            pieces.append((o, step, 0, wide_y))
            if o + step > 0:
                pieces.append(((wide_z - o) % wide_z, -step, 0, wide_y))
        plan.append(pieces)
    top = STRIDE * (levels - 1)
    plan[-1].append((top, STRIDE, 0, wide_y // 2))
    plan[-1].append(((wide_z - top) % wide_z, -STRIDE, wide_y // 2, wide_y))
    return plan


def tables(geo, sec, pairs, pair_target):
    wide_x, wide_y, wide_z = geo
    nblk = wide_z // 2
    half_z = wide_z // 2
    my_t = lax.axis_index("terms")
    my_s = lax.axis_index("sectors")
    my_z, my_y = my_s // wide_y, my_s % wide_y
    cells = sec * pairs
    slot_of, step_of = {}, {}
    for pieces in piece_plan(geo):
        for o, step, first, last in pieces:
            for yp in range(first, last):
                slot_of[(o + step) % wide_z, yp] = o
                step_of[(o + step) % wide_z, yp] = step
    keys = [(far, yp) for far in range(wide_z) for yp in range(wide_y)]
    slots = jnp.array([slot_of[key] for key in keys], jnp.int32)
    steps = jnp.array([step_of[key] for key in keys], jnp.int32)
    columns = jnp.array([yp for _, yp in keys], jnp.int32)
    readers = jnp.remainder(my_z + steps, wide_z) * wide_y + columns
    run = jnp.remainder(my_z - slots, wide_z) * wide_y + my_y
    asked = jnp.take(pair_target.reshape(wide_z * wide_y, cells), readers, axis=0)
    hit = asked // sec == run[:, None]
    wanted = jnp.sum(jnp.where(hit, asked % sec, 0), axis=1)
    own = lax.dynamic_slice_in_dim(pair_target, my_s * sec, sec, 0).reshape(cells)
    own_run = own // sec
    offset = jnp.remainder(my_z - own_run // wide_y, wide_z)
    holder = 2 * ((own_run % wide_y + my_y + offset) % wide_x) + offset // half_z
    slot = holder * nblk + offset % half_z
    chosen = slot[None, :] == (my_t * nblk + jnp.arange(nblk, dtype=jnp.int32))[:, None]
    cell = jnp.sum(jnp.where(chosen, jnp.arange(cells, dtype=jnp.int32)[None, :], 0), axis=1)
    target = jnp.sum(jnp.where(chosen, own[None, :], 0), axis=1)
    column = cell % pairs
    return jnp.concatenate([wanted, slot, cell // pairs, column // 2, column % 2, target])


def per_device(wide_y, wave, left_env, right_env, pair_target, block_dims):
    terms = lax.axis_size("terms")
    devices = lax.axis_size("sectors")
    geo = (terms // 2, wide_y, devices // wide_y)
    sec = wave.shape[0]
    pairs = wave.shape[2] // DB
    cells = sec * pairs
    nblk = geo[2] // 2
    plane = terms * wide_y
    chunks = 2
    tab = tables(geo, sec, pairs, pair_target)
    f32, bf16 = jnp.float32, jnp.bfloat16
    dma = pltpu.SemaphoreType.DMA
    vmem = pl.BlockSpec(memory_space=pltpu.VMEM)
    smem = pl.BlockSpec(memory_space=pltpu.SMEM)
    return pl.pallas_call(
        functools.partial(kernel, geo, cells),
        out_shape=(
            jax.ShapeDtypeStruct(wave.shape, f32),
            jax.ShapeDtypeStruct((2, 2), f32),
        ),
        in_specs=[smem, smem, pl.BlockSpec(memory_space=pl.ANY), vmem, vmem],
        out_specs=(vmem, vmem),
        scratch_shapes=[
            pltpu.VMEM(wave.shape, f32),
            pltpu.VMEM((geo[2], sec, HALF, LANES), f32),
            pltpu.VMEM((geo[2], wide_y, HALF, LANES), f32),
            pltpu.VMEM((nblk, terms, HALF, LANES), f32),
            pltpu.VMEM((terms, sec, HALF, LANES), f32),
            pltpu.VMEM((sec, terms * DB, LANES), bf16),
            pltpu.VMEM((LANES, terms * DB), bf16),
            pltpu.VMEM((LANES, terms * DB), bf16),
            pltpu.VMEM((terms, nblk, DB + 8, LANES), f32),
            pltpu.VMEM((plane, 1, LANES), f32),
            pltpu.VMEM((geo[2], 1, LANES), f32),
            dma,
            dma((geo[2], chunks)),
            dma((geo[2], chunks)),
            dma((geo[2], wide_y)),
            dma((nblk,)),
            dma((2 * geo[0] - 1,)),
            dma((terms,)),
            dma((plane,)),
            dma,
            dma((geo[2],)),
            dma,
            dma((nblk, geo[0])),
            dma((geo[0],)),
            dma((terms,)),
            pltpu.SemaphoreType.REGULAR,
            pltpu.SemaphoreType.REGULAR,
        ],
        compiler_params=pltpu.CompilerParams(
            collective_id=0, has_side_effects=True, vmem_limit_bytes=32 * 1024 * 1024
        ),
    )(
        tab,
        block_dims,
        wave,
        left_env.reshape(sec, DB * DB),
        right_env.reshape(sec, DB * DB),
    )


def solution(mesh, wide_y=WIDE_Y):
    in_specs = (
        P("sectors", None, None),
        P("terms", "sectors", None),
        P("terms", "sectors", None),
        P(),
        P(),
    )
    out_specs = (P("sectors", None, None), P())
    return jax.shard_map(
        functools.partial(per_device, wide_y),
        mesh=mesh,
        in_specs=in_specs,
        out_specs=out_specs,
        check_vma=False,
    )
```

```python
import functools

import jax
import jax.numpy as jnp
from jax import lax
from jax.experimental import pallas as pl
from jax.experimental.pallas import tpu as pltpu
from jax.sharding import PartitionSpec as P

MESH = pl.DeviceIdType.MESH
DB = 64
LANES = 128
HALF = DB // 2
WIDE_Y = 4
STRIDE = 2
TINY = 1e-30
NAMES = ("n", "c", "rr", "rf", "fg", "ri", "rg", "e")


def lane_low(rows):
    return lax.broadcasted_iota(jnp.int32, (rows, LANES), 1) < DB


def swap(x):
    return pltpu.roll(x, DB, 1)


def split(x):
    high = x.astype(jnp.bfloat16)
    low = (x - high.astype(jnp.float32)).astype(jnp.bfloat16)
    return high, low


def total(x):
    return jnp.sum(jnp.sum(x, axis=0, keepdims=True), axis=1, keepdims=True)


def recenter(stat, center):
    shift = stat["e"] - center
    return {
        "n": stat["n"],
        "c": stat["c"],
        "rr": stat["rr"] + 2.0 * shift * stat["rf"] + shift * shift * stat["n"],
        "rf": stat["rf"] + shift * stat["n"],
        "fg": stat["fg"] + shift * stat["c"],
        "ri": stat["ri"] + shift * stat["c"],
        "rg": stat["rg"] + shift * (stat["ri"] + stat["fg"]) + shift * shift * stat["c"],
    }


def quotient(cross, norm):
    return jnp.where(norm > TINY, cross / jnp.maximum(norm, TINY), 0.0)


def merge(stat, last):
    norm = jnp.sum(stat["n"], axis=0, keepdims=True)
    cross = jnp.sum(stat["c"], axis=0, keepdims=True)
    center = cross / norm if last else quotient(cross, norm)
    moved = recenter(stat, center)
    out = {name: jnp.sum(value, axis=0, keepdims=True) for name, value in moved.items()}
    out["e"] = center
    return out


def read_rows(buf):
    rows = buf[:, 0, :]
    return {name: rows[:, k : k + 1] for k, name in enumerate(NAMES)}


def row_of(stat):
    lane = lax.broadcasted_iota(jnp.int32, (1, LANES), 1)
    row = jnp.zeros((1, LANES), jnp.float32)
    for k, name in enumerate(NAMES):
        row = jnp.where(lane == k, stat[name], row)
    return row


def repack(src, dst):
    low = lane_low(src.shape[0])
    for u in range(HALF // 2):
        first = src[:, LANES * u : LANES * (u + 1)]
        second = src[:, LANES * (u + HALF // 2) : LANES * (u + HALF // 2 + 1)]
        dst[:, 2 * u, :] = jnp.where(low, first, swap(second))
        dst[:, 2 * u + 1, :] = jnp.where(low, swap(first), second)


def kernel(
    geo,
    wave_hbm,
    left_hbm,
    right_hbm,
    target_hbm,
    dims_hbm,
    out_ref,
    proj_ref,
    wave,
    left_ref,
    right_ref,
    target_ref,
    dims,
    asked,
    tab_vmem,
    tab,
    other,
    shifts,
    zbuf,
    stage,
    rrecv,
    lall,
    lbf,
    wcat,
    rcat,
    gbuf,
    red_a,
    red_b,
    in_sem,
    tab_sem,
    z_send,
    z_recv,
    p_send,
    p_recv,
    l_send,
    l_recv,
    a_send,
    a_recv,
    b_send,
    b_recv,
    g_send,
    g_pass,
    g_recv,
    plane_sem,
    space_sem,
):
    wide_x, wide_y, wide_z = geo
    terms = 2 * wide_x
    nblk = wide_z // 2
    half_z = wide_z // 2
    sec, pairs = wave.shape[0], wave.shape[2] // DB
    cells = sec * pairs
    chunks = z_send.shape[1]
    csec = sec // chunks
    plane = terms * wide_y

    my_t = lax.axis_index("terms")
    my_s = lax.axis_index("sectors")
    my_x = my_t // 2
    my_c = my_t % 2
    my_z = my_s // wide_y
    my_y = my_s % wide_y

    def dev(t, z, y):
        return {"terms": t, "sectors": z * wide_y + y}

    def plane_peer(i):
        other = lax.rem(my_t * wide_y + my_y + i, plane)
        return dev(other // wide_y, my_z, other % wide_y)

    def z_peer(i):
        return dev(my_t, lax.rem(my_z + i, wide_z), my_y)

    def y_peer(i):
        return dev(my_t, my_z, lax.rem(my_y + i, wide_y))

    def term_peer(i):
        return dev(lax.rem(my_t + i, terms), my_z, my_y)

    barrier = pltpu.get_barrier_semaphore()
    near = sorted({1, STRIDE, wide_z - STRIDE, wide_z - 1})

    def tell(sem, peers):
        for peer in peers:
            pl.semaphore_signal(sem, inc=1, device_id=peer, device_id_type=MESH)

    z_near = [z_peer(i) for i in near]
    y_near = [y_peer(i) for i in range(1, wide_y)]
    tell(barrier, z_near + y_near + [term_peer(i) for i in range(1, terms)])
    loads = [
        pltpu.make_async_copy(src, dst, in_sem.at[k])
        for k, (src, dst) in enumerate(
            (
                (right_hbm.at[0], right_ref),
                (left_hbm.at[0], left_ref),
                (target_hbm, target_ref),
                (dims_hbm, dims),
                (wave_hbm, wave),
            )
        )
    ]
    for load in loads:
        load.start()
    loads[0].wait()
    repack(right_ref, zbuf.at[0])
    loads[1].wait()
    repack(left_ref, lall.at[my_t])
    pl.semaphore_wait(barrier, len(near) + wide_y - 1 + terms - 1)

    def z_copy(src, dst, k, peer):
        part = pl.ds(k * csec, csec)
        return pltpu.make_async_remote_copy(
            src_ref=zbuf.at[src, part],
            dst_ref=zbuf.at[dst, part],
            send_sem=z_send.at[dst, k],
            recv_sem=z_recv.at[dst, k],
            device_id=peer,
            device_id_type=MESH,
        )

    up, down = z_peer(STRIDE), z_peer(wide_z - STRIDE)

    def forward_up(o, k):
        z_copy(o, o + STRIDE, k, up).start()

    def forward_down(o, k):
        z_copy(o, (o + wide_z - STRIDE) % wide_z, k, down).start()

    sibling = dev(my_t + 1 - 2 * my_c, my_z, my_y)

    def l_copy(t, peer, k):
        return pltpu.make_async_remote_copy(
            src_ref=lall.at[t],
            dst_ref=lall.at[t],
            send_sem=l_send.at[k],
            recv_sem=l_recv.at[t],
            device_id=peer,
            device_id_type=MESH,
        )

    def x_term(i):
        return lax.rem(my_x + i, wide_x) * 2 + my_c

    for k in range(chunks):
        forward_up(0, k)
        forward_down(0, k)
    for i in range(1, wide_x):
        l_copy(my_t, dev(x_term(i), my_z, my_y), i - 1).start()
    l_copy(my_t, sibling, wide_x - 1).start()

    tell(plane_sem, y_near)
    pl.semaphore_wait(plane_sem, wide_y - 1)
    tell(space_sem, z_near)

    plan = piece_plan(geo)
    for k in range(2, 5):
        loads[k].wait()
    width = min(LANES, target_ref.shape[1])
    sec_bits, y_bits = sec.bit_length() - 1, wide_y.bit_length() - 1
    tile_lane = lax.broadcasted_iota(jnp.int32, (pairs, width), 1)
    tile_row = lax.broadcasted_iota(jnp.int32, (pairs, width), 0)

    def run_tile(run):
        base = lax.div(run * sec, width) * width
        tile = target_ref[:, pl.ds(pl.multiple_of(base, width), width)]
        return tile, ((tile_lane + base) >> sec_bits) == run

    def ask(o, step, first, last):
        far = (o + step) % wide_z
        wanted = lax.rem(my_z + (wide_z - o), wide_z) * wide_y + my_y

        def one(yp, carry):
            reader = lax.rem(my_z + (wide_z + step), wide_z) * wide_y + yp
            tile, own = run_tile(reader)
            hit = jnp.logical_and(own, (tile >> sec_bits) == wanted)
            value = total(jnp.where(hit, (tile & (sec - 1)).astype(jnp.float32), 0.0))
            asked[far, yp] = jnp.broadcast_to(value, (8, LANES))
            return carry

        lax.fori_loop(first, last, one, 0)

    for pieces in plan:
        for one in pieces:
            ask(*one)
    tile, own = run_tile(my_s)
    run = tile >> sec_bits
    far = (my_z - (run >> y_bits) + wide_z) & (wide_z - 1)
    column = ((run & (wide_y - 1)) + my_y + far) & (wide_x - 1)
    slot = (2 * column + (far >> (half_z.bit_length() - 1))) * nblk + (far & (nblk - 1))
    tab_vmem[0:pairs, 0:width] = slot
    full_row = lax.broadcasted_iota(jnp.int32, (8, LANES), 0)
    full_lane = lax.broadcasted_iota(jnp.int32, (8, LANES), 1)
    found = jnp.zeros((8, LANES), jnp.float32)
    for b in range(nblk):
        hit = jnp.logical_and(own, slot == my_t * nblk + b)
        for k, what in enumerate((tile_lane & (sec - 1), tile_row, tile)):
            value = total(jnp.where(hit, what.astype(jnp.float32), 0.0))
            here = jnp.logical_and(full_row == b, full_lane == k)
            found = jnp.where(here, value, found)
    tab_vmem[8:16, :] = found.astype(jnp.int32)
    tab_copy = pltpu.make_async_copy(tab_vmem, tab, tab_sem)
    tab_copy.start()
    pl.semaphore_wait(space_sem, len(near))

    def owner(far, step, yp):
        t = 2 * lax.rem(my_y + yp + far, wide_x) + far // half_z
        if step != 0:
            return t, jnp.bool_(False)
        return t, jnp.logical_and(t == my_t, yp == my_y)

    def remote_piece(far, step, yp):
        t, _ = owner(far, step, yp)
        return pltpu.make_async_remote_copy(
            src_ref=stage.at[far, yp],
            dst_ref=rrecv.at[far % half_z, my_t],
            send_sem=p_send.at[far, yp],
            recv_sem=p_recv.at[far % half_z],
            device_id=dev(t, lax.rem(my_z + (wide_z + step), wide_z), yp),
            device_id_type=MESH,
        )

    def local_piece(far, yp):
        b = far % half_z
        return pltpu.make_async_copy(stage.at[far, yp], rrecv.at[b, my_t], p_recv.at[b])

    def hand_out(o, step, first, last):
        far = (o + step) % wide_z

        def one(yp, carry):
            wanted = asked[far, yp]
            picks = [wanted == k for k in range(1, sec)]
            for r in range(0, HALF, 8):
                got = zbuf[o, 0, r : r + 8]
                for k in range(1, sec):
                    got = jnp.where(picks[k - 1], zbuf[o, k, r : r + 8], got)
                stage[far, yp, r : r + 8] = got
            if step != 0:
                remote_piece(far, step, yp).start()
                return carry
            _, mine = owner(far, step, yp)

            @pl.when(mine)
            def _():
                local_piece(far, yp).start()

            @pl.when(jnp.logical_not(mine))
            def _():
                remote_piece(far, step, yp).start()

            return carry

        lax.fori_loop(first, last, one, 0)

    def sent(o, step, first, last):
        far = (o + step) % wide_z

        def one(yp, carry):
            if step != 0:
                remote_piece(far, step, yp).wait_send()
                return carry
            _, mine = owner(far, step, yp)

            @pl.when(jnp.logical_not(mine))
            def _():
                remote_piece(far, step, yp).wait_send()

            return carry

        lax.fori_loop(first, last, one, 0)

    def arrive(o, k):
        z_copy(o, o, k, up).wait_recv()

    def level(n):
        last = n == len(plan) - 1
        for k in range(chunks):
            arrive(STRIDE * n, k)
            if not last:
                forward_up(STRIDE * n, k)
            arrive(wide_z - STRIDE * n, k)
            if not last:
                forward_down(wide_z - STRIDE * n, k)
        for one in plan[n]:
            hand_out(*one)

    low64 = lane_low(DB)
    low32 = lane_low(HALF)
    lane = lax.broadcasted_iota(jnp.int32, (DB, LANES), 1)
    row = lax.broadcasted_iota(jnp.int32, (DB, LANES), 0)

    both_now = range(2)

    def apply(vecs, qs):
        rhs = []
        for k in both_now:
            vh, vl = split(vecs[k])
            rhs.append(jnp.concatenate([vh, vh, vl, vl], axis=0))
        for u in range(terms // 2):
            for k in both_now:
                lhs = lbf[qs[k], u * LANES : (u + 1) * LANES, :]
                part = jnp.dot(
                    jnp.concatenate([lhs, lhs], axis=1), rhs[k], preferred_element_type=jnp.float32
                )
                high, low = split(jnp.where(low64, part[:DB], part[DB:]))
                wcat[k, :DB, u * LANES : (u + 1) * LANES] = high
                wcat[k, DB:, u * LANES : (u + 1) * LANES] = low
        outs = []
        for k in both_now:
            out = lax.dot_general(
                wcat[k], rcat[k], (((1,), (1,)), ((), ())), preferred_element_type=jnp.float32
            )
            out = out[:DB] + out[DB:]
            outs.append(out + swap(out))
        return outs

    def pack(x):
        return jnp.where(low32, x[:HALF], x[HALF:])

    def work(m):
        low_b = jnp.where(my_c == 0, 2 * m, nblk - 2 - 2 * m)
        bs = [low_b, low_b + 1]
        for b in bs:
            pltpu.make_async_copy(rrecv.at[b], rrecv.at[b], p_recv.at[b]).wait()
        for k, b in enumerate(bs):
            for u in range(terms // 2):
                first, second = rrecv[b, 2 * u], rrecv[b, 2 * u + 1]
                top = jnp.where(low32, first, swap(second))
                bottom = jnp.where(low32, swap(first), second)
                high, low = split(jnp.concatenate([top, bottom], axis=0))
                rcat[k, :DB, u * LANES : (u + 1) * LANES] = high
                rcat[k, DB:, u * LANES : (u + 1) * LANES] = low
        qs, useds, firsts = [], [], []
        for b in bs:
            q, j = tab[8 + b, 0] & (sec - 1), tab[8 + b, 1]
            target = tab[8 + b, 2] & (dims.shape[0] - 1)
            column = jnp.full((DB, LANES), j >> 1, jnp.int32)
            odd = jnp.full((DB, LANES), j & 1, jnp.int32)
            raw = wave[q, :, 0:LANES]
            for u in range(1, pairs // 2):
                raw = jnp.where(column == u, wave[q, :, u * LANES : (u + 1) * LANES], raw)
            raw = jnp.where((lane >> 6) == odd, raw, swap(raw))
            used = jnp.logical_and(row < dims[my_s * sec + q], (lane & (DB - 1)) < dims[target])
            qs.append(q)
            useds.append(used)
            firsts.append(jnp.where(used, raw, 0.0))
        images = [jnp.where(useds[k], x, 0.0) for k, x in enumerate(apply(firsts, qs))]
        norms = [0.5 * total(firsts[k] * firsts[k]) for k in both_now]
        crosses = [0.5 * total(firsts[k] * images[k]) for k in both_now]
        energies = [quotient(crosses[k], norms[k]) for k in both_now]
        rests = [images[k] - energies[k] * firsts[k] for k in both_now]
        seconds = [jnp.where(useds[k], x, 0.0) for k, x in enumerate(apply(rests, qs))]
        sub = lax.broadcasted_iota(jnp.int32, (8, LANES), 0)
        for k, b in enumerate(bs):
            first, image, rest, second = firsts[k], images[k], rests[k], seconds[k]
            gbuf[my_t, b, :HALF] = pack(second)
            gbuf[my_t, b, HALF:DB] = pack(image)
            values = (
                norms[k],
                crosses[k],
                0.5 * total(rest * rest),
                0.5 * total(rest * first),
                0.5 * total(first * second),
                0.5 * total(rest * image),
                0.5 * total(rest * second),
                energies[k],
            )
            tile = jnp.zeros((8, LANES), jnp.float32)
            for n, value in enumerate(values):
                tile = jnp.where(sub == n, value, tile)
            gbuf[my_t, b, DB:] = tile
        for i in far_first(wide_x):
            g_pair(low_b, i - 1, dev(x_term(i), my_z, my_y)).start()
        g_pair(low_b, wide_x - 1, sibling).start()

    def g_pair(b, k, peer):
        return pltpu.make_async_remote_copy(
            src_ref=gbuf.at[my_t, pl.ds(b, 2)],
            dst_ref=gbuf.at[my_t, pl.ds(b, 2)],
            send_sem=g_send.at[b // 2, k],
            recv_sem=g_recv.at[my_t],
            device_id=peer,
            device_id_type=MESH,
        )

    def g_copy(t, k, peer):
        return pltpu.make_async_remote_copy(
            src_ref=gbuf.at[t],
            dst_ref=gbuf.at[t],
            send_sem=g_pass.at[k],
            recv_sem=g_recv.at[t],
            device_id=peer,
            device_id_type=MESH,
        )

    def unpack_left():
        def one(t, carry):
            for q in range(sec):
                x = lall[t, q]
                high, low = split(x)
                high, low = high.astype(jnp.float32), low.astype(jnp.float32)
                top = jnp.where(low32, high, swap(low))
                bottom = jnp.where(low32, swap(high), low)
                both = jnp.concatenate([top, bottom], axis=0).astype(jnp.bfloat16)
                lbf[q, pl.ds(pl.multiple_of(t * DB, DB), DB), :] = both
            return carry

        lax.fori_loop(0, terms, one, 0)

    for one in plan[0]:
        hand_out(*one)
    levels = len(plan) - 1
    for n in range(1, levels + 1):
        level(n)
        if n == 1:
            for i in range(1, wide_x):
                t = x_term(i)
                l_copy(t, sibling, 0).wait_recv()
                l_copy(t, sibling, wide_x - 1 + i).start()
            tab_copy.wait()
        if n == min(2, levels):
            for i in range(wide_x):
                l_copy(lax.rem(my_x + i, wide_x) * 2 + 1 - my_c, sibling, 0).wait_recv()
            unpack_left()
            if levels > 2:
                lax.fori_loop(0, 2, lambda m, c: (work(m), c)[1], 0)
    lax.fori_loop(2 if levels > 2 else 0, nblk // 2, lambda m, c: (work(m), c)[1], 0)

    stat = {name: gbuf[my_t, :, DB + k, :] for k, name in enumerate(NAMES)}
    mine = my_t * wide_y + my_y
    red_a[mine] = row_of(merge(stat, False))

    def a_copy(i):
        return pltpu.make_async_remote_copy(
            src_ref=red_a.at[mine],
            dst_ref=red_a.at[mine],
            send_sem=a_send.at[i],
            recv_sem=a_recv,
            device_id=plane_peer(i),
            device_id_type=MESH,
        )

    def b_copy(i):
        return pltpu.make_async_remote_copy(
            src_ref=red_b.at[my_z],
            dst_ref=red_b.at[my_z],
            send_sem=b_send.at[i],
            recv_sem=b_recv,
            device_id=z_peer(i),
            device_id_type=MESH,
        )

    lax.fori_loop(1, plane, lambda i, c: (a_copy(i).start(), c)[1], 0)
    for i in range(1, wide_x):
        t = x_term(i)
        g_copy(t, i - 1, sibling).wait_recv()
        g_copy(t, i - 1, sibling).start()
    pltpu.make_async_copy(
        red_a.at[pl.ds(0, plane - 1)], red_a.at[pl.ds(0, plane - 1)], a_recv
    ).wait()
    red_b[my_z] = row_of(merge(read_rows(red_a), False))
    for i in far_first(wide_z):
        b_copy(i).start()
    for i in range(wide_x):
        g_copy(lax.rem(my_x + i, wide_x) * 2 + 1 - my_c, 0, sibling).wait_recv()

    def place(q, carry):
        for u in range(pairs // 2):
            ats = [tab[2 * u + k, lax.rem(my_s * sec, width) + q] for k in range(2)]
            parts = [(at // nblk, lax.rem(at, nblk)) for at in ats]
            for dst, lo in ((out_ref, 0), (other, HALF)):
                first, second = [gbuf[t, b, lo : lo + HALF] for t, b in parts]
                dst[q, 0:HALF, u * LANES : (u + 1) * LANES] = jnp.where(
                    low32, first, swap(second)
                )
                dst[q, HALF:DB, u * LANES : (u + 1) * LANES] = jnp.where(
                    low32, swap(first), second
                )
            first, second = [gbuf[t, b, DB : DB + 8] for t, b in parts]
            shifts[q, :, u * LANES : (u + 1) * LANES] = jnp.where(low32[:8], first, second)
        return carry

    lax.fori_loop(0, sec, place, 0)

    for n in range(len(plan) - 1):
        for k in range(chunks):
            z_copy(0, STRIDE * (n + 1), k, up).wait_send()
            z_copy(0, wide_z - STRIDE * (n + 1), k, down).wait_send()
    for pieces in plan:
        for one in pieces:
            sent(*one)
    for i in range(2 * wide_x - 1):
        l_copy(my_t, sibling, i).wait_send()

    def g_done(b, carry):
        for k in range(wide_x):
            g_pair(2 * b, k, sibling).wait_send()
        return carry

    lax.fori_loop(0, nblk // 2, g_done, 0)
    for i in range(wide_x - 1):
        g_copy(my_t, i, sibling).wait_send()
    lax.fori_loop(1, plane, lambda i, c: (a_copy(i).wait_send(), c)[1], 0)
    pltpu.make_async_copy(
        red_b.at[pl.ds(0, wide_z - 1)], red_b.at[pl.ds(0, wide_z - 1)], b_recv
    ).wait()
    final = merge(read_rows(red_b), True)
    cell_total = float(plane * wide_z * nblk * DB * DB)
    squared = jnp.maximum(final["rr"], 0.0)
    scale = 1.0 / jnp.sqrt(squared / cell_total + 1e-06)
    sub2 = lax.broadcasted_iota(jnp.int32, (2, 2), 0)
    lane2 = lax.broadcasted_iota(jnp.int32, (2, 2), 1)
    proj_ref[...] = (
        jnp.where(
            sub2 == 0,
            jnp.where(lane2 == 0, final["c"], final["fg"] * scale),
            jnp.where(lane2 == 0, final["ri"] * scale, final["rg"] * scale * scale),
        )
        / cell_total
    )

    def finish(q, carry):
        shift = shifts[q, 7:8, :] - final["e"]
        out_ref[q] = (out_ref[q] + shift * other[q]) * scale
        return carry

    lax.fori_loop(0, sec, finish, 0)

    lax.fori_loop(1, wide_z, lambda i, c: (b_copy(i).wait_send(), c)[1], 0)


def far_first(count):
    return sorted(range(1, count), key=lambda i: -min(i, count - i))


def piece_plan(geo):
    _, wide_y, wide_z = geo
    levels = wide_z // (2 * STRIDE)
    plan = []
    for n in range(levels):
        o = STRIDE * n
        pieces = []
        for step in range(STRIDE):
            pieces.append((o, step, 0, wide_y))
            if o + step > 0:
                pieces.append(((wide_z - o) % wide_z, -step, 0, wide_y))
        plan.append(pieces)
    top = STRIDE * (levels - 1)
    plan[-1].append((top, STRIDE, 0, wide_y // 2))
    plan[-1].append(((wide_z - top) % wide_z, -STRIDE, wide_y // 2, wide_y))
    return plan


def per_device(wide_y, wave, left_env, right_env, pair_target, block_dims):
    terms = lax.axis_size("terms")
    devices = lax.axis_size("sectors")
    geo = (terms // 2, wide_y, devices // wide_y)
    sec = wave.shape[0]
    pairs = wave.shape[2] // DB
    nblk = geo[2] // 2
    plane = terms * wide_y
    chunks = 4
    f32, bf16 = jnp.float32, jnp.bfloat16
    dma = pltpu.SemaphoreType.DMA
    vmem = pl.BlockSpec(memory_space=pltpu.VMEM)
    return pl.pallas_call(
        functools.partial(kernel, geo),
        out_shape=(
            jax.ShapeDtypeStruct(wave.shape, f32),
            jax.ShapeDtypeStruct((2, 2), f32),
        ),
        in_specs=[pl.BlockSpec(memory_space=pl.ANY)] * 5,
        out_specs=(vmem, vmem),
        scratch_shapes=[
            pltpu.VMEM(wave.shape, f32),
            pltpu.VMEM((sec, DB * DB), f32),
            pltpu.VMEM((sec, DB * DB), f32),
            pltpu.VMEM((pairs, pair_target.shape[0]), jnp.int32),
            pltpu.SMEM(block_dims.shape, jnp.int32),
            pltpu.VMEM((geo[2], wide_y, 8, LANES), f32),
            pltpu.VMEM((16, LANES), jnp.int32),
            pltpu.SMEM((16, LANES), jnp.int32),
            pltpu.VMEM(wave.shape, f32),
            pltpu.VMEM((sec, 8, pairs * DB), f32),
            pltpu.VMEM((geo[2], sec, HALF, LANES), f32),
            pltpu.VMEM((geo[2], wide_y, HALF, LANES), f32),
            pltpu.VMEM((nblk, terms, HALF, LANES), f32),
            pltpu.VMEM((terms, sec, HALF, LANES), f32),
            pltpu.VMEM((sec, terms * DB, LANES), bf16),
            pltpu.VMEM((2, LANES, terms * DB), bf16),
            pltpu.VMEM((2, LANES, terms * DB), bf16),
            pltpu.VMEM((terms, nblk, DB + 8, LANES), f32),
            pltpu.VMEM((plane, 1, LANES), f32),
            pltpu.VMEM((geo[2], 1, LANES), f32),
            dma((5,)),
            dma,
            dma((geo[2], chunks)),
            dma((geo[2], chunks)),
            dma((geo[2], wide_y)),
            dma((nblk,)),
            dma((2 * geo[0] - 1,)),
            dma((terms,)),
            dma((plane,)),
            dma,
            dma((geo[2],)),
            dma,
            dma((nblk // 2, geo[0])),
            dma((geo[0],)),
            dma((terms,)),
            pltpu.SemaphoreType.REGULAR,
            pltpu.SemaphoreType.REGULAR,
        ],
        compiler_params=pltpu.CompilerParams(
            collective_id=0, has_side_effects=True, vmem_limit_bytes=56 * 1024 * 1024
        ),
    )(
        wave,
        left_env,
        right_env,
        pair_target.T,
        block_dims,
    )


def solution(mesh, wide_y=WIDE_Y):
    in_specs = (
        P("sectors", None, None),
        P("terms", "sectors", None),
        P("terms", "sectors", None),
        P(),
        P(),
    )
    out_specs = (P("sectors", None, None), P())
    return jax.shard_map(
        functools.partial(per_device, wide_y),
        mesh=mesh,
        in_specs=in_specs,
        out_specs=out_specs,
        check_vma=False,
    )
```

```python
import functools

import jax
import jax.numpy as jnp
from jax import lax
from jax.experimental import pallas as pl
from jax.experimental.pallas import tpu as pltpu
from jax.sharding import PartitionSpec as P

MESH = pl.DeviceIdType.MESH
DB = 64
LANES = 128
HALF = DB // 2
WIDE_Y = 4
STRIDE = 2
TINY = 1e-30
NAMES = ("n", "c", "rr", "rf", "fg", "ri", "rg", "e")


def lane_low(rows):
    return lax.broadcasted_iota(jnp.int32, (rows, LANES), 1) < DB


def swap(x):
    return pltpu.roll(x, DB, 1)


def split(x):
    high = x.astype(jnp.bfloat16)
    low = (x - high.astype(jnp.float32)).astype(jnp.bfloat16)
    return high, low


def total(x):
    return jnp.sum(jnp.sum(x, axis=0, keepdims=True), axis=1, keepdims=True)


def recenter(stat, center):
    shift = stat["e"] - center
    return {
        "n": stat["n"],
        "c": stat["c"],
        "rr": stat["rr"] + 2.0 * shift * stat["rf"] + shift * shift * stat["n"],
        "rf": stat["rf"] + shift * stat["n"],
        "fg": stat["fg"] + shift * stat["c"],
        "ri": stat["ri"] + shift * stat["c"],
        "rg": stat["rg"] + shift * (stat["ri"] + stat["fg"]) + shift * shift * stat["c"],
    }


def quotient(cross, norm):
    return jnp.where(norm > TINY, cross / jnp.maximum(norm, TINY), 0.0)


def merge(stat, last):
    norm = jnp.sum(stat["n"], axis=0, keepdims=True)
    cross = jnp.sum(stat["c"], axis=0, keepdims=True)
    center = cross / norm if last else quotient(cross, norm)
    moved = recenter(stat, center)
    out = {name: jnp.sum(value, axis=0, keepdims=True) for name, value in moved.items()}
    out["e"] = center
    return out


def read_rows(buf):
    rows = buf[:, 0, :]
    return {name: rows[:, k : k + 1] for k, name in enumerate(NAMES)}


def row_of(stat):
    lane = lax.broadcasted_iota(jnp.int32, (1, LANES), 1)
    row = jnp.zeros((1, LANES), jnp.float32)
    for k, name in enumerate(NAMES):
        row = jnp.where(lane == k, stat[name], row)
    return row


def repack(src, dst):
    low = lane_low(src.shape[0])
    for u in range(HALF // 2):
        first = src[:, LANES * u : LANES * (u + 1)]
        second = src[:, LANES * (u + HALF // 2) : LANES * (u + HALF // 2 + 1)]
        dst[:, 2 * u, :] = jnp.where(low, first, swap(second))
        dst[:, 2 * u + 1, :] = jnp.where(low, swap(first), second)


def kernel(
    geo,
    wave_hbm,
    left_hbm,
    right_hbm,
    target_hbm,
    dims_hbm,
    second_ref,
    first_ref,
    shift_ref,
    sums_ref,
    proj_ref,
    wave,
    left_ref,
    right_ref,
    target_ref,
    dims,
    asked,
    tab_vmem,
    tab,
    ready,
    other,
    shifts,
    zbuf,
    stage,
    rrecv,
    lall,
    lbf,
    wcat,
    rcat,
    gbuf,
    red_a,
    red_b,
    in_sem,
    out_sem,
    tab_sem,
    z_send,
    z_recv,
    p_send,
    p_recv,
    l_send,
    l_recv,
    a_send,
    a_recv,
    b_send,
    b_recv,
    g_send,
    g_pass,
    g_recv,
    plane_sem,
    space_sem,
):
    wide_x, wide_y, wide_z = geo
    terms = 2 * wide_x
    nblk = wide_z // 2
    half_z = wide_z // 2
    sec, pairs = wave.shape[0], wave.shape[2] // DB
    cells = sec * pairs
    chunks = z_send.shape[1]
    csec = sec // chunks
    plane = terms * wide_y

    my_t = lax.axis_index("terms")
    my_s = lax.axis_index("sectors")
    my_x = my_t // 2
    my_c = my_t % 2
    my_z = my_s // wide_y
    my_y = my_s % wide_y

    def dev(t, z, y):
        return {"terms": t, "sectors": z * wide_y + y}

    def plane_peer(i):
        other = lax.rem(my_t * wide_y + my_y + i, plane)
        return dev(other // wide_y, my_z, other % wide_y)

    def z_peer(i):
        return dev(my_t, lax.rem(my_z + i, wide_z), my_y)

    def y_peer(i):
        return dev(my_t, my_z, lax.rem(my_y + i, wide_y))

    def term_peer(i):
        return dev(lax.rem(my_t + i, terms), my_z, my_y)

    barrier = pltpu.get_barrier_semaphore()
    near = sorted({1, STRIDE, wide_z - STRIDE, wide_z - 1})

    def tell(sem, peers):
        for peer in peers:
            pl.semaphore_signal(sem, inc=1, device_id=peer, device_id_type=MESH)

    z_near = [z_peer(i) for i in near]
    y_near = [y_peer(i) for i in range(1, wide_y)]
    loads = [
        pltpu.make_async_copy(src, dst, in_sem.at[k])
        for k, (src, dst) in enumerate(
            (
                (right_hbm.at[0], right_ref),
                (left_hbm.at[0], left_ref),
                (target_hbm, target_ref),
                (dims_hbm, dims),
                (wave_hbm, wave),
            )
        )
    ]
    for load in loads:
        load.start()
    tell(barrier, z_near + y_near + [term_peer(i) for i in range(1, terms)])
    loads[0].wait()
    repack(right_ref, zbuf.at[0])
    pl.semaphore_wait(barrier, len(near) + wide_y - 1 + terms - 1)

    def z_copy(src, dst, k, peer):
        part = pl.ds(k * csec, csec)
        return pltpu.make_async_remote_copy(
            src_ref=zbuf.at[src, part],
            dst_ref=zbuf.at[dst, part],
            send_sem=z_send.at[dst, k],
            recv_sem=z_recv.at[dst, k],
            device_id=peer,
            device_id_type=MESH,
        )

    up, down = z_peer(STRIDE), z_peer(wide_z - STRIDE)

    def forward_up(o, k):
        z_copy(o, o + STRIDE, k, up).start()

    def forward_down(o, k):
        z_copy(o, (o + wide_z - STRIDE) % wide_z, k, down).start()

    sibling = dev(my_t + 1 - 2 * my_c, my_z, my_y)

    def l_copy(t, peer, k):
        return pltpu.make_async_remote_copy(
            src_ref=lall.at[t],
            dst_ref=lall.at[t],
            send_sem=l_send.at[k],
            recv_sem=l_recv.at[t],
            device_id=peer,
            device_id_type=MESH,
        )

    def x_term(i):
        return lax.rem(my_x + i, wide_x) * 2 + my_c

    for k in range(chunks):
        forward_up(0, k)
        forward_down(0, k)
    loads[1].wait()
    repack(left_ref, lall.at[my_t])
    for i in range(1, wide_x):
        l_copy(my_t, dev(x_term(i), my_z, my_y), i - 1).start()
    l_copy(my_t, sibling, wide_x - 1).start()

    tell(plane_sem, y_near)

    plan = piece_plan(geo)
    for k in range(2, 5):
        loads[k].wait()
    width = min(LANES, target_ref.shape[1])
    sec_bits, y_bits = sec.bit_length() - 1, wide_y.bit_length() - 1
    tile_lane = lax.broadcasted_iota(jnp.int32, (pairs, width), 1)
    tile_row = lax.broadcasted_iota(jnp.int32, (pairs, width), 0)

    def run_tile(run):
        base = lax.div(run * sec, width) * width
        tile = target_ref[:, pl.ds(pl.multiple_of(base, width), width)]
        return tile, ((tile_lane + base) >> sec_bits) == run

    def ask(o, step, first, last):
        far = (o + step) % wide_z
        wanted = lax.rem(my_z + (wide_z - o), wide_z) * wide_y + my_y

        def one(yp):
            reader = lax.rem(my_z + (wide_z + step), wide_z) * wide_y + yp
            tile, own = run_tile(reader)
            hit = jnp.logical_and(own, (tile >> sec_bits) == wanted)
            value = total(jnp.where(hit, (tile & (sec - 1)).astype(jnp.float32), 0.0))
            asked[far, yp] = jnp.broadcast_to(value, (8, LANES))

        for yp in range(first, last):
            one(yp)

    for pieces in plan:
        for one in pieces:
            ask(*one)
    tile, own = run_tile(my_s)
    run = tile >> sec_bits
    far = (my_z - (run >> y_bits) + wide_z) & (wide_z - 1)
    column = ((run & (wide_y - 1)) + my_y + far) & (wide_x - 1)
    slot = (2 * column + (far >> (half_z.bit_length() - 1))) * nblk + (far & (nblk - 1))
    tab_vmem[0:pairs, 0:width] = slot
    full_row = lax.broadcasted_iota(jnp.int32, (8, LANES), 0)
    full_lane = lax.broadcasted_iota(jnp.int32, (8, LANES), 1)
    found = jnp.zeros((8, LANES), jnp.float32)
    for b in range(nblk):
        hit = jnp.logical_and(own, slot == my_t * nblk + b)
        for k, what in enumerate((tile_lane & (sec - 1), tile_row, tile)):
            value = total(jnp.where(hit, what.astype(jnp.float32), 0.0))
            here = jnp.logical_and(full_row == b, full_lane == k)
            found = jnp.where(here, value, found)
    tab_vmem[8:16, :] = found.astype(jnp.int32)
    tab_copy = pltpu.make_async_copy(tab_vmem, tab, tab_sem)
    tab_copy.start()
    pl.semaphore_wait(plane_sem, wide_y - 1)
    tell(space_sem, z_near)

    def owner(far, step, yp):
        t = 2 * lax.rem(my_y + yp + far, wide_x) + far // half_z
        if step != 0:
            return t, jnp.bool_(False)
        return t, jnp.logical_and(t == my_t, yp == my_y)

    def remote_piece(far, step, yp):
        t, _ = owner(far, step, yp)
        return pltpu.make_async_remote_copy(
            src_ref=stage.at[far, yp],
            dst_ref=rrecv.at[far % half_z, my_t],
            send_sem=p_send.at[far, yp],
            recv_sem=p_recv.at[far % half_z],
            device_id=dev(t, lax.rem(my_z + (wide_z + step), wide_z), yp),
            device_id_type=MESH,
        )

    def local_piece(far, yp):
        b = far % half_z
        return pltpu.make_async_copy(stage.at[far, yp], rrecv.at[b, my_t], p_recv.at[b])

    def hand_out(o, step, first, last):
        far = (o + step) % wide_z

        def one(yp, carry):
            wanted = asked[far, yp]
            picks = [wanted == k for k in range(1, sec)]
            for r in range(0, HALF, 8):
                got = zbuf[o, 0, r : r + 8]
                for k in range(1, sec):
                    got = jnp.where(picks[k - 1], zbuf[o, k, r : r + 8], got)
                stage[far, yp, r : r + 8] = got
            if step != 0:
                remote_piece(far, step, yp).start()
                return carry
            _, mine = owner(far, step, yp)

            @pl.when(mine)
            def _():
                local_piece(far, yp).start()

            @pl.when(jnp.logical_not(mine))
            def _():
                remote_piece(far, step, yp).start()

            return carry

        lax.fori_loop(first, last, one, 0)

    def sent(o, step, first, last):
        far = (o + step) % wide_z

        def one(yp, carry):
            if step != 0:
                remote_piece(far, step, yp).wait_send()
                return carry
            _, mine = owner(far, step, yp)

            @pl.when(jnp.logical_not(mine))
            def _():
                remote_piece(far, step, yp).wait_send()

            return carry

        lax.fori_loop(first, last, one, 0)

    def arrive(o, k):
        z_copy(o, o, k, up).wait_recv()

    levels = len(plan) - 1

    def relay(n):
        for k in range(chunks):
            arrive(STRIDE * n, k)
            if n < levels:
                forward_up(STRIDE * n, k)
            arrive(wide_z - STRIDE * n, k)
            if n < levels:
                forward_down(wide_z - STRIDE * n, k)

    def pass_on(n):
        for one in sorted(plan[n], key=lambda piece: -abs(piece[1])):
            hand_out(*one)

    low64 = lane_low(DB)
    low32 = lane_low(HALF)
    lane = lax.broadcasted_iota(jnp.int32, (DB, LANES), 1)
    row = lax.broadcasted_iota(jnp.int32, (DB, LANES), 0)

    both_now = range(2)

    def apply(vecs, qs):
        rhs = []
        for k in both_now:
            vh, vl = split(vecs[k])
            rhs.append(jnp.concatenate([vh, vh, vl, vl], axis=0))
        for u in range(terms // 2):
            for k in both_now:
                lhs = lbf[qs[k], u * LANES : (u + 1) * LANES, :]
                part = jnp.dot(
                    jnp.concatenate([lhs, lhs], axis=1), rhs[k], preferred_element_type=jnp.float32
                )
                high, low = split(jnp.where(low64, part[:DB], part[DB:]))
                wcat[k, :DB, u * LANES : (u + 1) * LANES] = high
                wcat[k, DB:, u * LANES : (u + 1) * LANES] = low
        outs = []
        for k in both_now:
            out = lax.dot_general(
                wcat[k], rcat[k], (((1,), (1,)), ((), ())), preferred_element_type=jnp.float32
            )
            out = out[:DB] + out[DB:]
            outs.append(out + swap(out))
        return outs

    def pack(x):
        return jnp.where(low32, x[:HALF], x[HALF:])

    def work(m):
        low_b = jnp.where(my_c == 0, 2 * m, nblk - 2 - 2 * m)
        bs = [low_b, low_b + 1]
        for b in bs:
            pltpu.make_async_copy(rrecv.at[b], rrecv.at[b], p_recv.at[b]).wait()
        for k, b in enumerate(bs):
            for u in range(terms // 2):
                first, second = rrecv[b, 2 * u], rrecv[b, 2 * u + 1]
                top = jnp.where(low32, first, swap(second))
                bottom = jnp.where(low32, swap(first), second)
                high, low = split(jnp.concatenate([top, bottom], axis=0))
                rcat[k, :DB, u * LANES : (u + 1) * LANES] = high
                rcat[k, DB:, u * LANES : (u + 1) * LANES] = low
        qs, useds, firsts = [], [], []
        for b in bs:
            q, j = tab[8 + b, 0] & (sec - 1), tab[8 + b, 1]
            target = tab[8 + b, 2] & (dims.shape[0] - 1)
            column = jnp.full((DB, LANES), j >> 1, jnp.int32)
            odd = jnp.full((DB, LANES), j & 1, jnp.int32)
            raw = wave[q, :, 0:LANES]
            for u in range(1, pairs // 2):
                raw = jnp.where(column == u, wave[q, :, u * LANES : (u + 1) * LANES], raw)
            raw = jnp.where((lane >> 6) == odd, raw, swap(raw))
            used = jnp.logical_and(row < dims[my_s * sec + q], (lane & (DB - 1)) < dims[target])
            qs.append(q)
            useds.append(used)
            firsts.append(jnp.where(used, raw, 0.0))
        images = [jnp.where(useds[k], x, 0.0) for k, x in enumerate(apply(firsts, qs))]
        norms = [0.5 * total(firsts[k] * firsts[k]) for k in both_now]
        crosses = [0.5 * total(firsts[k] * images[k]) for k in both_now]
        energies = [quotient(crosses[k], norms[k]) for k in both_now]
        rests = [images[k] - energies[k] * firsts[k] for k in both_now]
        seconds = [jnp.where(useds[k], x, 0.0) for k, x in enumerate(apply(rests, qs))]
        sub = lax.broadcasted_iota(jnp.int32, (8, LANES), 0)
        for k, b in enumerate(bs):
            first, image, rest, second = firsts[k], images[k], rests[k], seconds[k]
            gbuf[my_t, b, :HALF] = pack(second)
            gbuf[my_t, b, HALF:DB] = pack(image)
            values = (
                norms[k],
                crosses[k],
                0.5 * total(rest * rest),
                0.5 * total(rest * first),
                0.5 * total(first * second),
                0.5 * total(rest * image),
                0.5 * total(rest * second),
                energies[k],
            )
            tile = jnp.zeros((8, LANES), jnp.float32)
            for n, value in enumerate(values):
                tile = jnp.where(sub == n, value, tile)
            gbuf[my_t, b, DB:] = tile
        return low_b

    def send_pair(low_b):
        for i in far_first(wide_x):
            g_pair(low_b, i - 1, dev(x_term(i), my_z, my_y)).start()
        g_pair(low_b, wide_x - 1, sibling).start()

    def g_pair(b, k, peer):
        return pltpu.make_async_remote_copy(
            src_ref=gbuf.at[my_t, pl.ds(b, 2)],
            dst_ref=gbuf.at[my_t, pl.ds(b, 2)],
            send_sem=g_send.at[b // 2, k],
            recv_sem=g_recv.at[my_t],
            device_id=peer,
            device_id_type=MESH,
        )

    def g_copy(t, k, peer):
        return pltpu.make_async_remote_copy(
            src_ref=gbuf.at[t],
            dst_ref=gbuf.at[t],
            send_sem=g_pass.at[k],
            recv_sem=g_recv.at[t],
            device_id=peer,
            device_id_type=MESH,
        )

    def unpack_left():
        def one(t, carry):
            for q in range(sec):
                x = lall[t, q]
                high, low = split(x)
                high, low = high.astype(jnp.float32), low.astype(jnp.float32)
                top = jnp.where(low32, high, swap(low))
                bottom = jnp.where(low32, swap(high), low)
                both = jnp.concatenate([top, bottom], axis=0).astype(jnp.bfloat16)
                lbf[q, pl.ds(pl.multiple_of(t * DB, DB), DB), :] = both
            return carry

        lax.fori_loop(0, terms, one, 0)

    for n in range(1, levels + 1):
        relay(n)
        if n == 1:
            pl.semaphore_wait(space_sem, len(near))
            pass_on(0)
        pass_on(n)
        if n == 1:
            for i in range(1, wide_x):
                t = x_term(i)
                l_copy(t, sibling, 0).wait_recv()
                l_copy(t, sibling, wide_x - 1 + i).start()
            tab_copy.wait()
        if n == min(2, levels):
            for i in range(wide_x):
                l_copy(lax.rem(my_x + i, wide_x) * 2 + 1 - my_c, sibling, 0).wait_recv()
            unpack_left()
            send_pair(work(0))
    for m in range(1, nblk // 2 - 1):
        send_pair(work(m))
    last_pair = work(nblk // 2 - 1)

    stat = {name: gbuf[my_t, :, DB + k, :] for k, name in enumerate(NAMES)}
    mine = my_t * wide_y + my_y
    red_b[my_z] = row_of(merge(stat, False))

    def a_copy(i):
        return pltpu.make_async_remote_copy(
            src_ref=red_a.at[mine],
            dst_ref=red_a.at[mine],
            send_sem=a_send.at[i],
            recv_sem=a_recv,
            device_id=plane_peer(i),
            device_id_type=MESH,
        )

    def b_copy(i):
        return pltpu.make_async_remote_copy(
            src_ref=red_b.at[my_z],
            dst_ref=red_b.at[my_z],
            send_sem=b_send.at[i],
            recv_sem=b_recv,
            device_id=z_peer(i),
            device_id_type=MESH,
        )

    for i in far_first(wide_z):
        b_copy(i).start()
    send_pair(last_pair)
    pltpu.make_async_copy(
        red_b.at[pl.ds(0, wide_z - 1)], red_b.at[pl.ds(0, wide_z - 1)], b_recv
    ).wait()
    red_a[mine] = row_of(merge(read_rows(red_b), False))
    lax.fori_loop(1, plane, lambda i, c: (a_copy(i).start(), c)[1], 0)
    for i in range(1, wide_x):
        t = x_term(i)
        g_copy(t, i - 1, sibling).wait_recv()
        g_copy(t, i - 1, sibling).start()
    for i in range(wide_x):
        g_copy(lax.rem(my_x + i, wide_x) * 2 + 1 - my_c, 0, sibling).wait_recv()

    def place(q, carry):
        for u in range(pairs // 2):
            ats = [tab[2 * u + k, lax.rem(my_s * sec, width) + q] for k in range(2)]
            parts = [(at // nblk, lax.rem(at, nblk)) for at in ats]
            for dst, lo in ((ready, 0), (other, HALF)):
                first, second = [gbuf[t, b, lo : lo + HALF] for t, b in parts]
                dst[q, 0:HALF, u * LANES : (u + 1) * LANES] = jnp.where(
                    low32, first, swap(second)
                )
                dst[q, HALF:DB, u * LANES : (u + 1) * LANES] = jnp.where(
                    low32, swap(first), second
                )
            first, second = [gbuf[t, b, DB : DB + 8] for t, b in parts]
            shifts[q, :, u * LANES : (u + 1) * LANES] = jnp.where(low32[:8], first, second)
        return carry

    lax.fori_loop(0, sec, place, 0)
    stores = [
        pltpu.make_async_copy(src, dst, out_sem.at[k])
        for k, (src, dst) in enumerate(((ready, second_ref), (other, first_ref), (shifts, shift_ref)))
    ]
    for store in stores:
        store.start()

    for n in range(len(plan) - 1):
        for k in range(chunks):
            z_copy(0, STRIDE * (n + 1), k, up).wait_send()
            z_copy(0, wide_z - STRIDE * (n + 1), k, down).wait_send()
    for pieces in plan:
        for one in pieces:
            sent(*one)
    for i in range(2 * wide_x - 1):
        l_copy(my_t, sibling, i).wait_send()

    def g_done(b, carry):
        for k in range(wide_x):
            g_pair(2 * b, k, sibling).wait_send()
        return carry

    lax.fori_loop(0, nblk // 2, g_done, 0)
    for i in range(wide_x - 1):
        g_copy(my_t, i, sibling).wait_send()
    lax.fori_loop(1, wide_z, lambda i, c: (b_copy(i).wait_send(), c)[1], 0)
    pltpu.make_async_copy(
        red_a.at[pl.ds(0, plane - 1)], red_a.at[pl.ds(0, plane - 1)], a_recv
    ).wait()
    final = merge(read_rows(red_a), True)
    cell_total = float(plane * wide_z * nblk * DB * DB)
    squared = jnp.maximum(final["rr"], 0.0)
    scale = 1.0 / jnp.sqrt(squared / cell_total + 1e-06)
    sub2 = lax.broadcasted_iota(jnp.int32, (2, 2), 0)
    lane2 = lax.broadcasted_iota(jnp.int32, (2, 2), 1)
    proj_ref[...] = (
        jnp.where(
            sub2 == 0,
            jnp.where(lane2 == 0, final["c"], final["fg"] * scale),
            jnp.where(lane2 == 0, final["ri"] * scale, final["rg"] * scale * scale),
        )
        / cell_total
    )

    sub8 = lax.broadcasted_iota(jnp.int32, (8, LANES), 0)
    sums_ref[...] = jnp.where(sub8 == 0, final["e"], scale)
    for store in stores:
        store.wait()
    lax.fori_loop(1, plane, lambda i, c: (a_copy(i).wait_send(), c)[1], 0)


def far_first(count):
    return sorted(range(1, count), key=lambda i: -min(i, count - i))


def piece_plan(geo):
    _, wide_y, wide_z = geo
    levels = wide_z // (2 * STRIDE)
    plan = []
    for n in range(levels):
        o = STRIDE * n
        pieces = []
        for step in range(STRIDE):
            pieces.append((o, step, 0, wide_y))
            if o + step > 0:
                pieces.append(((wide_z - o) % wide_z, -step, 0, wide_y))
        plan.append(pieces)
    top = STRIDE * (levels - 1)
    plan[-1].append((top, STRIDE, 0, wide_y // 2))
    plan[-1].append(((wide_z - top) % wide_z, -STRIDE, wide_y // 2, wide_y))
    return plan


def per_device(wide_y, wave, left_env, right_env, pair_target, block_dims):
    terms = lax.axis_size("terms")
    devices = lax.axis_size("sectors")
    geo = (terms // 2, wide_y, devices // wide_y)
    sec = wave.shape[0]
    pairs = wave.shape[2] // DB
    nblk = geo[2] // 2
    plane = terms * wide_y
    chunks = 4
    f32, bf16 = jnp.float32, jnp.bfloat16
    dma = pltpu.SemaphoreType.DMA
    vmem = pl.BlockSpec(memory_space=pltpu.VMEM)
    hbm = pl.BlockSpec(memory_space=pl.ANY)
    second, first, shift, sums, projected = pl.pallas_call(
        functools.partial(kernel, geo),
        out_shape=(
            jax.ShapeDtypeStruct(wave.shape, f32),
            jax.ShapeDtypeStruct(wave.shape, f32),
            jax.ShapeDtypeStruct((sec, 8, pairs * DB), f32),
            jax.ShapeDtypeStruct((8, LANES), f32),
            jax.ShapeDtypeStruct((2, 2), f32),
        ),
        in_specs=[hbm] * 5,
        out_specs=(hbm, hbm, hbm, vmem, vmem),
        scratch_shapes=[
            pltpu.VMEM(wave.shape, f32),
            pltpu.VMEM((sec, DB * DB), f32),
            pltpu.VMEM((sec, DB * DB), f32),
            pltpu.VMEM((pairs, pair_target.shape[0]), jnp.int32),
            pltpu.SMEM(block_dims.shape, jnp.int32),
            pltpu.VMEM((geo[2], wide_y, 8, LANES), f32),
            pltpu.VMEM((16, LANES), jnp.int32),
            pltpu.SMEM((16, LANES), jnp.int32),
            pltpu.VMEM(wave.shape, f32),
            pltpu.VMEM(wave.shape, f32),
            pltpu.VMEM((sec, 8, pairs * DB), f32),
            pltpu.VMEM((geo[2], sec, HALF, LANES), f32),
            pltpu.VMEM((geo[2], wide_y, HALF, LANES), f32),
            pltpu.VMEM((nblk, terms, HALF, LANES), f32),
            pltpu.VMEM((terms, sec, HALF, LANES), f32),
            pltpu.VMEM((sec, terms * DB, LANES), bf16),
            pltpu.VMEM((2, LANES, terms * DB), bf16),
            pltpu.VMEM((2, LANES, terms * DB), bf16),
            pltpu.VMEM((terms, nblk, DB + 8, LANES), f32),
            pltpu.VMEM((plane, 1, LANES), f32),
            pltpu.VMEM((geo[2], 1, LANES), f32),
            dma((5,)),
            dma((3,)),
            dma,
            dma((geo[2], chunks)),
            dma((geo[2], chunks)),
            dma((geo[2], wide_y)),
            dma((nblk,)),
            dma((2 * geo[0] - 1,)),
            dma((terms,)),
            dma((plane,)),
            dma,
            dma((geo[2],)),
            dma,
            dma((nblk // 2, geo[0])),
            dma((geo[0],)),
            dma((terms,)),
            pltpu.SemaphoreType.REGULAR,
            pltpu.SemaphoreType.REGULAR,
        ],
        compiler_params=pltpu.CompilerParams(
            collective_id=0, has_side_effects=True, vmem_limit_bytes=56 * 1024 * 1024
        ),
    )(
        wave,
        left_env,
        right_env,
        pair_target.T,
        block_dims,
    )
    image_two = (second + (shift[:, 7:8, :] - sums[0, 0]) * first) * sums[1, 0]
    return image_two, projected


def solution(mesh, wide_y=WIDE_Y):
    in_specs = (
        P("sectors", None, None),
        P("terms", "sectors", None),
        P("terms", "sectors", None),
        P(),
        P(),
    )
    out_specs = (P("sectors", None, None), P())
    return jax.shard_map(
        functools.partial(per_device, wide_y),
        mesh=mesh,
        in_specs=in_specs,
        out_specs=out_specs,
        check_vma=False,
    )
```

```python
import functools

import jax
import jax.numpy as jnp
from jax import lax
from jax.experimental import pallas as pl
from jax.experimental.pallas import tpu as pltpu
from jax.sharding import PartitionSpec as P

MESH = pl.DeviceIdType.MESH
DB = 64
LANES = 128
HALF = DB // 2
WIDE_Y = 4
STRIDE = 2
TINY = 1e-30
NAMES = ("n", "c", "rr", "rf", "fg", "ri", "rg", "e")


def lane_low(rows):
    return lax.broadcasted_iota(jnp.int32, (rows, LANES), 1) < DB


def swap(x):
    return pltpu.roll(x, DB, 1)


def split(x):
    high = x.astype(jnp.bfloat16)
    low = (x - high.astype(jnp.float32)).astype(jnp.bfloat16)
    return high, low


def total(x):
    return jnp.sum(jnp.sum(x, axis=0, keepdims=True), axis=1, keepdims=True)


def recenter(stat, center):
    shift = stat["e"] - center
    return {
        "n": stat["n"],
        "c": stat["c"],
        "rr": stat["rr"] + 2.0 * shift * stat["rf"] + shift * shift * stat["n"],
        "rf": stat["rf"] + shift * stat["n"],
        "fg": stat["fg"] + shift * stat["c"],
        "ri": stat["ri"] + shift * stat["c"],
        "rg": stat["rg"] + shift * (stat["ri"] + stat["fg"]) + shift * shift * stat["c"],
    }


def quotient(cross, norm):
    return jnp.where(norm > TINY, cross / jnp.maximum(norm, TINY), 0.0)


def merge(stat, last):
    norm = jnp.sum(stat["n"], axis=0, keepdims=True)
    cross = jnp.sum(stat["c"], axis=0, keepdims=True)
    center = cross / norm if last else quotient(cross, norm)
    moved = recenter(stat, center)
    out = {name: jnp.sum(value, axis=0, keepdims=True) for name, value in moved.items()}
    out["e"] = center
    return out


def read_rows(buf):
    rows = buf[:, 0, :]
    return {name: rows[:, k : k + 1] for k, name in enumerate(NAMES)}


def row_of(stat):
    lane = lax.broadcasted_iota(jnp.int32, (1, LANES), 1)
    row = jnp.zeros((1, LANES), jnp.float32)
    for k, name in enumerate(NAMES):
        row = jnp.where(lane == k, stat[name], row)
    return row


def repack(src, dst):
    low = lane_low(src.shape[0])
    for u in range(HALF // 2):
        first = src[:, LANES * u : LANES * (u + 1)]
        second = src[:, LANES * (u + HALF // 2) : LANES * (u + HALF // 2 + 1)]
        dst[:, 2 * u, :] = jnp.where(low, first, swap(second))
        dst[:, 2 * u + 1, :] = jnp.where(low, swap(first), second)


def kernel(
    geo,
    wave_hbm,
    left_hbm,
    right_hbm,
    target_hbm,
    dims_hbm,
    out_ref,
    proj_ref,
    wave,
    left_ref,
    right_ref,
    target_ref,
    dims,
    asked,
    tab_vmem,
    tab,
    ready,
    other,
    shifts,
    zbuf,
    stage,
    rrecv,
    lall,
    lbf,
    wcat,
    rcat,
    gbuf,
    red_a,
    red_b,
    in_sem,
    out_sem,
    tab_sem,
    z_send,
    z_recv,
    p_send,
    p_recv,
    l_send,
    l_recv,
    a_send,
    a_recv,
    b_send,
    b_recv,
    g_send,
    g_pass,
    g_recv,
    plane_sem,
    space_sem,
):
    wide_x, wide_y, wide_z = geo
    terms = 2 * wide_x
    nblk = wide_z // 2
    half_z = wide_z // 2
    sec, pairs = wave.shape[0], wave.shape[2] // DB
    cells = sec * pairs
    chunks = z_send.shape[1]
    csec = sec // chunks
    plane = terms * wide_y

    my_t = lax.axis_index("terms")
    my_s = lax.axis_index("sectors")
    my_x = my_t // 2
    my_c = my_t % 2
    my_z = my_s // wide_y
    my_y = my_s % wide_y

    def dev(t, z, y):
        return {"terms": t, "sectors": z * wide_y + y}

    def plane_peer(i):
        other = lax.rem(my_t * wide_y + my_y + i, plane)
        return dev(other // wide_y, my_z, other % wide_y)

    def z_peer(i):
        return dev(my_t, lax.rem(my_z + i, wide_z), my_y)

    def y_peer(i):
        return dev(my_t, my_z, lax.rem(my_y + i, wide_y))

    def term_peer(i):
        return dev(lax.rem(my_t + i, terms), my_z, my_y)

    barrier = pltpu.get_barrier_semaphore()
    near = sorted({1, STRIDE, wide_z - STRIDE, wide_z - 1})

    def tell(sem, peers):
        for peer in peers:
            pl.semaphore_signal(sem, inc=1, device_id=peer, device_id_type=MESH)

    z_near = [z_peer(i) for i in near]
    y_near = [y_peer(i) for i in range(1, wide_y)]
    loads = [
        pltpu.make_async_copy(src, dst, in_sem.at[k])
        for k, (src, dst) in enumerate(
            (
                (right_hbm.at[0], right_ref),
                (left_hbm.at[0], left_ref),
                (target_hbm, target_ref),
                (dims_hbm, dims),
                (wave_hbm, wave),
            )
        )
    ]
    for load in loads:
        load.start()
    tell(barrier, z_near + y_near + [term_peer(i) for i in range(1, terms)])
    loads[0].wait()
    repack(right_ref, zbuf.at[0])
    pl.semaphore_wait(barrier, len(near) + wide_y - 1 + terms - 1)

    def z_copy(src, dst, k, peer):
        part = pl.ds(k * csec, csec)
        return pltpu.make_async_remote_copy(
            src_ref=zbuf.at[src, part],
            dst_ref=zbuf.at[dst, part],
            send_sem=z_send.at[dst, k],
            recv_sem=z_recv.at[dst, k],
            device_id=peer,
            device_id_type=MESH,
        )

    up, down = z_peer(STRIDE), z_peer(wide_z - STRIDE)

    def forward_up(o, k):
        z_copy(o, o + STRIDE, k, up).start()

    def forward_down(o, k):
        z_copy(o, (o + wide_z - STRIDE) % wide_z, k, down).start()

    sibling = dev(my_t + 1 - 2 * my_c, my_z, my_y)

    def l_copy(t, peer, k):
        return pltpu.make_async_remote_copy(
            src_ref=lall.at[t],
            dst_ref=lall.at[t],
            send_sem=l_send.at[k],
            recv_sem=l_recv.at[t],
            device_id=peer,
            device_id_type=MESH,
        )

    def x_term(i):
        return lax.rem(my_x + i, wide_x) * 2 + my_c

    for k in range(chunks):
        forward_up(0, k)
        forward_down(0, k)
    loads[1].wait()
    repack(left_ref, lall.at[my_t])
    for i in range(1, wide_x):
        l_copy(my_t, dev(x_term(i), my_z, my_y), i - 1).start()
    l_copy(my_t, sibling, wide_x - 1).start()

    tell(plane_sem, y_near)

    plan = piece_plan(geo)
    for k in range(2, 5):
        loads[k].wait()
    width = min(LANES, target_ref.shape[1])
    sec_bits, y_bits = sec.bit_length() - 1, wide_y.bit_length() - 1
    tile_lane = lax.broadcasted_iota(jnp.int32, (pairs, width), 1)
    tile_row = lax.broadcasted_iota(jnp.int32, (pairs, width), 0)

    def run_tile(run):
        base = lax.div(run * sec, width) * width
        tile = target_ref[:, pl.ds(pl.multiple_of(base, width), width)]
        return tile, ((tile_lane + base) >> sec_bits) == run

    def ask(o, step, first, last):
        far = (o + step) % wide_z
        wanted = lax.rem(my_z + (wide_z - o), wide_z) * wide_y + my_y

        def one(yp):
            reader = lax.rem(my_z + (wide_z + step), wide_z) * wide_y + yp
            tile, own = run_tile(reader)
            hit = jnp.logical_and(own, (tile >> sec_bits) == wanted)
            value = total(jnp.where(hit, (tile & (sec - 1)).astype(jnp.float32), 0.0))
            asked[far, yp] = jnp.broadcast_to(value, (8, LANES))

        for yp in range(first, last):
            one(yp)

    for pieces in plan:
        for one in pieces:
            ask(*one)
    tile, own = run_tile(my_s)
    run = tile >> sec_bits
    far = (my_z - (run >> y_bits) + wide_z) & (wide_z - 1)
    column = ((run & (wide_y - 1)) + my_y + far) & (wide_x - 1)
    slot = (2 * column + (far >> (half_z.bit_length() - 1))) * nblk + (far & (nblk - 1))
    tab_vmem[0:pairs, 0:width] = slot
    full_row = lax.broadcasted_iota(jnp.int32, (8, LANES), 0)
    full_lane = lax.broadcasted_iota(jnp.int32, (8, LANES), 1)
    found = jnp.zeros((8, LANES), jnp.float32)
    for b in range(nblk):
        hit = jnp.logical_and(own, slot == my_t * nblk + b)
        for k, what in enumerate((tile_lane & (sec - 1), tile_row, tile)):
            value = total(jnp.where(hit, what.astype(jnp.float32), 0.0))
            here = jnp.logical_and(full_row == b, full_lane == k)
            found = jnp.where(here, value, found)
    tab_vmem[8:16, :] = found.astype(jnp.int32)
    tab_copy = pltpu.make_async_copy(tab_vmem, tab, tab_sem)
    tab_copy.start()
    pl.semaphore_wait(plane_sem, wide_y - 1)
    tell(space_sem, z_near)

    def owner(far, step, yp):
        t = 2 * lax.rem(my_y + yp + far, wide_x) + far // half_z
        if step != 0:
            return t, jnp.bool_(False)
        return t, jnp.logical_and(t == my_t, yp == my_y)

    def remote_piece(far, step, yp):
        t, _ = owner(far, step, yp)
        return pltpu.make_async_remote_copy(
            src_ref=stage.at[far, yp],
            dst_ref=rrecv.at[far % half_z, my_t],
            send_sem=p_send.at[far, yp],
            recv_sem=p_recv.at[far % half_z],
            device_id=dev(t, lax.rem(my_z + (wide_z + step), wide_z), yp),
            device_id_type=MESH,
        )

    def local_piece(far, yp):
        b = far % half_z
        return pltpu.make_async_copy(stage.at[far, yp], rrecv.at[b, my_t], p_recv.at[b])

    def hand_out(o, step, first, last):
        far = (o + step) % wide_z

        def one(yp, carry):
            wanted = asked[far, yp]
            picks = [wanted == k for k in range(1, sec)]
            for r in range(0, HALF, 8):
                got = zbuf[o, 0, r : r + 8]
                for k in range(1, sec):
                    got = jnp.where(picks[k - 1], zbuf[o, k, r : r + 8], got)
                stage[far, yp, r : r + 8] = got
            if step != 0:
                remote_piece(far, step, yp).start()
                return carry
            _, mine = owner(far, step, yp)

            @pl.when(mine)
            def _():
                local_piece(far, yp).start()

            @pl.when(jnp.logical_not(mine))
            def _():
                remote_piece(far, step, yp).start()

            return carry

        lax.fori_loop(first, last, one, 0)

    def sent(o, step, first, last):
        far = (o + step) % wide_z

        def one(yp, carry):
            if step != 0:
                remote_piece(far, step, yp).wait_send()
                return carry
            _, mine = owner(far, step, yp)

            @pl.when(jnp.logical_not(mine))
            def _():
                remote_piece(far, step, yp).wait_send()

            return carry

        lax.fori_loop(first, last, one, 0)

    def arrive(o, k):
        z_copy(o, o, k, up).wait_recv()

    levels = len(plan) - 1

    def relay(n):
        for k in range(chunks):
            arrive(STRIDE * n, k)
            if n < levels:
                forward_up(STRIDE * n, k)
            arrive(wide_z - STRIDE * n, k)
            if n < levels:
                forward_down(wide_z - STRIDE * n, k)

    def pass_on(n):
        for one in sorted(plan[n], key=lambda piece: -abs(piece[1])):
            hand_out(*one)

    low64 = lane_low(DB)
    low32 = lane_low(HALF)
    lane = lax.broadcasted_iota(jnp.int32, (DB, LANES), 1)
    row = lax.broadcasted_iota(jnp.int32, (DB, LANES), 0)

    both_now = range(2)

    def apply(vecs, qs):
        rhs = []
        for k in both_now:
            vh, vl = split(vecs[k])
            rhs.append(jnp.concatenate([vh, vh, vl, vl], axis=0))
        for u in range(terms // 2):
            for k in both_now:
                lhs = lbf[qs[k], u * LANES : (u + 1) * LANES, :]
                part = jnp.dot(
                    jnp.concatenate([lhs, lhs], axis=1), rhs[k], preferred_element_type=jnp.float32
                )
                high, low = split(jnp.where(low64, part[:DB], part[DB:]))
                wcat[k, :DB, u * LANES : (u + 1) * LANES] = high
                wcat[k, DB:, u * LANES : (u + 1) * LANES] = low
        outs = []
        for k in both_now:
            out = lax.dot_general(
                wcat[k], rcat[k], (((1,), (1,)), ((), ())), preferred_element_type=jnp.float32
            )
            out = out[:DB] + out[DB:]
            outs.append(out + swap(out))
        return outs

    def pack(x):
        return jnp.where(low32, x[:HALF], x[HALF:])

    def work(m):
        low_b = jnp.where(my_c == 0, 2 * m, nblk - 2 - 2 * m)
        bs = [low_b, low_b + 1]
        for b in bs:
            pltpu.make_async_copy(rrecv.at[b], rrecv.at[b], p_recv.at[b]).wait()
        for k, b in enumerate(bs):
            for u in range(terms // 2):
                first, second = rrecv[b, 2 * u], rrecv[b, 2 * u + 1]
                top = jnp.where(low32, first, swap(second))
                bottom = jnp.where(low32, swap(first), second)
                high, low = split(jnp.concatenate([top, bottom], axis=0))
                rcat[k, :DB, u * LANES : (u + 1) * LANES] = high
                rcat[k, DB:, u * LANES : (u + 1) * LANES] = low
        qs, useds, firsts = [], [], []
        for b in bs:
            q, j = tab[8 + b, 0] & (sec - 1), tab[8 + b, 1]
            target = tab[8 + b, 2] & (dims.shape[0] - 1)
            column = jnp.full((DB, LANES), j >> 1, jnp.int32)
            odd = jnp.full((DB, LANES), j & 1, jnp.int32)
            raw = wave[q, :, 0:LANES]
            for u in range(1, pairs // 2):
                raw = jnp.where(column == u, wave[q, :, u * LANES : (u + 1) * LANES], raw)
            raw = jnp.where((lane >> 6) == odd, raw, swap(raw))
            used = jnp.logical_and(row < dims[my_s * sec + q], (lane & (DB - 1)) < dims[target])
            qs.append(q)
            useds.append(used)
            firsts.append(jnp.where(used, raw, 0.0))
        images = [jnp.where(useds[k], x, 0.0) for k, x in enumerate(apply(firsts, qs))]
        norms = [0.5 * total(firsts[k] * firsts[k]) for k in both_now]
        crosses = [0.5 * total(firsts[k] * images[k]) for k in both_now]
        energies = [quotient(crosses[k], norms[k]) for k in both_now]
        rests = [images[k] - energies[k] * firsts[k] for k in both_now]
        seconds = [jnp.where(useds[k], x, 0.0) for k, x in enumerate(apply(rests, qs))]
        sub = lax.broadcasted_iota(jnp.int32, (8, LANES), 0)
        for k, b in enumerate(bs):
            first, image, rest, second = firsts[k], images[k], rests[k], seconds[k]
            gbuf[my_t, b, :HALF] = pack(second)
            gbuf[my_t, b, HALF:DB] = pack(image)
            values = (
                norms[k],
                crosses[k],
                0.5 * total(rest * rest),
                0.5 * total(rest * first),
                0.5 * total(first * second),
                0.5 * total(rest * image),
                0.5 * total(rest * second),
                energies[k],
            )
            tile = jnp.zeros((8, LANES), jnp.float32)
            for n, value in enumerate(values):
                tile = jnp.where(sub == n, value, tile)
            gbuf[my_t, b, DB:] = tile
        return low_b

    def send_pair(low_b):
        for i in far_first(wide_x):
            g_pair(low_b, i - 1, dev(x_term(i), my_z, my_y)).start()
        g_pair(low_b, wide_x - 1, sibling).start()

    def g_pair(b, k, peer):
        return pltpu.make_async_remote_copy(
            src_ref=gbuf.at[my_t, pl.ds(b, 2)],
            dst_ref=gbuf.at[my_t, pl.ds(b, 2)],
            send_sem=g_send.at[b // 2, k],
            recv_sem=g_recv.at[my_t, b // 2],
            device_id=peer,
            device_id_type=MESH,
        )

    def g_copy(t, b, k, peer):
        return pltpu.make_async_remote_copy(
            src_ref=gbuf.at[t, pl.ds(b, 2)],
            dst_ref=gbuf.at[t, pl.ds(b, 2)],
            send_sem=g_pass.at[b // 2, k],
            recv_sem=g_recv.at[t, b // 2],
            device_id=peer,
            device_id_type=MESH,
        )

    def pass_pair(m):
        low_b = jnp.where(my_c == 0, 2 * m, nblk - 2 - 2 * m)
        for i in range(1, wide_x):
            g_copy(x_term(i), low_b, i - 1, sibling).wait_recv()
            g_copy(x_term(i), low_b, i - 1, sibling).start()

    def unpack_left():
        def one(t, carry):
            for q in range(sec):
                x = lall[t, q]
                high, low = split(x)
                high, low = high.astype(jnp.float32), low.astype(jnp.float32)
                top = jnp.where(low32, high, swap(low))
                bottom = jnp.where(low32, swap(high), low)
                both = jnp.concatenate([top, bottom], axis=0).astype(jnp.bfloat16)
                lbf[q, pl.ds(pl.multiple_of(t * DB, DB), DB), :] = both
            return carry

        lax.fori_loop(0, terms, one, 0)

    for n in range(1, levels + 1):
        relay(n)
        if n == 1:
            pl.semaphore_wait(space_sem, len(near))
            pass_on(0)
        pass_on(n)
        if n == min(2, levels):
            for i in range(1, wide_x):
                t = x_term(i)
                l_copy(t, sibling, 0).wait_recv()
                l_copy(t, sibling, wide_x - 1 + i).start()
    tab_copy.wait()
    for i in range(wide_x):
        l_copy(lax.rem(my_x + i, wide_x) * 2 + 1 - my_c, sibling, 0).wait_recv()
    unpack_left()
    for m in range(nblk // 2 - 1):
        send_pair(work(m))
    last_pair = work(nblk // 2 - 1)

    stat = {name: gbuf[my_t, :, DB + k, :] for k, name in enumerate(NAMES)}
    mine = my_t * wide_y + my_y
    red_b[my_z] = row_of(merge(stat, False))

    def a_copy(i):
        return pltpu.make_async_remote_copy(
            src_ref=red_a.at[mine],
            dst_ref=red_a.at[mine],
            send_sem=a_send.at[i],
            recv_sem=a_recv,
            device_id=plane_peer(i),
            device_id_type=MESH,
        )

    def b_copy(i):
        return pltpu.make_async_remote_copy(
            src_ref=red_b.at[my_z],
            dst_ref=red_b.at[my_z],
            send_sem=b_send.at[i],
            recv_sem=b_recv,
            device_id=z_peer(i),
            device_id_type=MESH,
        )

    for i in far_first(wide_z):
        b_copy(i).start()
    send_pair(last_pair)
    for m in range(nblk // 2 - 1):
        pass_pair(m)
    pltpu.make_async_copy(
        red_b.at[pl.ds(0, wide_z - 1)], red_b.at[pl.ds(0, wide_z - 1)], b_recv
    ).wait()
    red_a[mine] = row_of(merge(read_rows(red_b), False))
    lax.fori_loop(1, plane, lambda i, c: (a_copy(i).start(), c)[1], 0)
    pass_pair(nblk // 2 - 1)
    for m in range(nblk // 2):
        for i in range(wide_x):
            g_copy(lax.rem(my_x + i, wide_x) * 2 + 1 - my_c, 2 * m, 0, sibling).wait_recv()

    def place(q, carry):
        for u in range(pairs // 2):
            ats = [tab[2 * u + k, lax.rem(my_s * sec, width) + q] for k in range(2)]
            parts = [(at // nblk, lax.rem(at, nblk)) for at in ats]
            for dst, lo in ((ready, 0), (other, HALF)):
                first, second = [gbuf[t, b, lo : lo + HALF] for t, b in parts]
                dst[q, 0:HALF, u * LANES : (u + 1) * LANES] = jnp.where(
                    low32, first, swap(second)
                )
                dst[q, HALF:DB, u * LANES : (u + 1) * LANES] = jnp.where(
                    low32, swap(first), second
                )
            first, second = [gbuf[t, b, DB : DB + 8] for t, b in parts]
            shifts[q, :, u * LANES : (u + 1) * LANES] = jnp.where(low32[:8], first, second)
        return carry

    lax.fori_loop(0, sec, place, 0)

    for n in range(len(plan) - 1):
        for k in range(chunks):
            z_copy(0, STRIDE * (n + 1), k, up).wait_send()
            z_copy(0, wide_z - STRIDE * (n + 1), k, down).wait_send()
    for pieces in plan:
        for one in pieces:
            sent(*one)
    for i in range(2 * wide_x - 1):
        l_copy(my_t, sibling, i).wait_send()

    def g_done(b, carry):
        for k in range(wide_x):
            g_pair(2 * b, k, sibling).wait_send()
        return carry

    lax.fori_loop(0, nblk // 2, g_done, 0)
    for m in range(nblk // 2):
        for i in range(wide_x - 1):
            g_copy(my_t, 2 * m, i, sibling).wait_send()
    lax.fori_loop(1, wide_z, lambda i, c: (b_copy(i).wait_send(), c)[1], 0)
    pltpu.make_async_copy(
        red_a.at[pl.ds(0, plane - 1)], red_a.at[pl.ds(0, plane - 1)], a_recv
    ).wait()
    final = merge(read_rows(red_a), True)
    cell_total = float(plane * wide_z * nblk * DB * DB)
    squared = jnp.maximum(final["rr"], 0.0)
    scale = 1.0 / jnp.sqrt(squared / cell_total + 1e-06)
    sub2 = lax.broadcasted_iota(jnp.int32, (2, 2), 0)
    lane2 = lax.broadcasted_iota(jnp.int32, (2, 2), 1)
    proj_ref[...] = (
        jnp.where(
            sub2 == 0,
            jnp.where(lane2 == 0, final["c"], final["fg"] * scale),
            jnp.where(lane2 == 0, final["ri"] * scale, final["rg"] * scale * scale),
        )
        / cell_total
    )

    for q in range(sec):
        shift = shifts[q, 7:8, :] - final["e"][:, :1]
        ready[q] = (ready[q] + shift * other[q]) * scale
        pltpu.make_async_copy(ready.at[q], out_ref.at[q], out_sem.at[q]).start()
    lax.fori_loop(1, plane, lambda i, c: (a_copy(i).wait_send(), c)[1], 0)
    for q in range(sec):
        pltpu.make_async_copy(ready.at[q], out_ref.at[q], out_sem.at[q]).wait()


def far_first(count):
    return sorted(range(1, count), key=lambda i: -min(i, count - i))


def piece_plan(geo):
    _, wide_y, wide_z = geo
    levels = wide_z // (2 * STRIDE)
    plan = []
    for n in range(levels):
        o = STRIDE * n
        pieces = []
        for step in range(STRIDE):
            pieces.append((o, step, 0, wide_y))
            if o + step > 0:
                pieces.append(((wide_z - o) % wide_z, -step, 0, wide_y))
        plan.append(pieces)
    top = STRIDE * (levels - 1)
    plan[-1].append((top, STRIDE, 0, wide_y // 2))
    plan[-1].append(((wide_z - top) % wide_z, -STRIDE, wide_y // 2, wide_y))
    return plan


def per_device(wide_y, wave, left_env, right_env, pair_target, block_dims):
    terms = lax.axis_size("terms")
    devices = lax.axis_size("sectors")
    geo = (terms // 2, wide_y, devices // wide_y)
    sec = wave.shape[0]
    pairs = wave.shape[2] // DB
    nblk = geo[2] // 2
    plane = terms * wide_y
    chunks = 4
    f32, bf16 = jnp.float32, jnp.bfloat16
    dma = pltpu.SemaphoreType.DMA
    vmem = pl.BlockSpec(memory_space=pltpu.VMEM)
    hbm = pl.BlockSpec(memory_space=pl.ANY)
    return pl.pallas_call(
        functools.partial(kernel, geo),
        out_shape=(
            jax.ShapeDtypeStruct(wave.shape, f32),
            jax.ShapeDtypeStruct((2, 2), f32),
        ),
        in_specs=[hbm] * 5,
        out_specs=(hbm, vmem),
        scratch_shapes=[
            pltpu.VMEM(wave.shape, f32),
            pltpu.VMEM((sec, DB * DB), f32),
            pltpu.VMEM((sec, DB * DB), f32),
            pltpu.VMEM((pairs, pair_target.shape[0]), jnp.int32),
            pltpu.SMEM(block_dims.shape, jnp.int32),
            pltpu.VMEM((geo[2], wide_y, 8, LANES), f32),
            pltpu.VMEM((16, LANES), jnp.int32),
            pltpu.SMEM((16, LANES), jnp.int32),
            pltpu.VMEM(wave.shape, f32),
            pltpu.VMEM(wave.shape, f32),
            pltpu.VMEM((sec, 8, pairs * DB), f32),
            pltpu.VMEM((geo[2], sec, HALF, LANES), f32),
            pltpu.VMEM((geo[2], wide_y, HALF, LANES), f32),
            pltpu.VMEM((nblk, terms, HALF, LANES), f32),
            pltpu.VMEM((terms, sec, HALF, LANES), f32),
            pltpu.VMEM((sec, terms * DB, LANES), bf16),
            pltpu.VMEM((2, LANES, terms * DB), bf16),
            pltpu.VMEM((2, LANES, terms * DB), bf16),
            pltpu.VMEM((terms, nblk, DB + 8, LANES), f32),
            pltpu.VMEM((plane, 1, LANES), f32),
            pltpu.VMEM((geo[2], 1, LANES), f32),
            dma((5,)),
            dma((sec,)),
            dma,
            dma((geo[2], chunks)),
            dma((geo[2], chunks)),
            dma((geo[2], wide_y)),
            dma((nblk,)),
            dma((2 * geo[0] - 1,)),
            dma((terms,)),
            dma((plane,)),
            dma,
            dma((geo[2],)),
            dma,
            dma((nblk // 2, geo[0])),
            dma((nblk // 2, geo[0])),
            dma((terms, nblk // 2)),
            pltpu.SemaphoreType.REGULAR,
            pltpu.SemaphoreType.REGULAR,
        ],
        compiler_params=pltpu.CompilerParams(
            collective_id=0, has_side_effects=True, vmem_limit_bytes=56 * 1024 * 1024
        ),
    )(
        wave,
        left_env,
        right_env,
        pair_target.T,
        block_dims,
    )


def solution(mesh, wide_y=WIDE_Y):
    in_specs = (
        P("sectors", None, None),
        P("terms", "sectors", None),
        P("terms", "sectors", None),
        P(),
        P(),
    )
    out_specs = (P("sectors", None, None), P())
    return jax.shard_map(
        functools.partial(per_device, wide_y),
        mesh=mesh,
        in_specs=in_specs,
        out_specs=out_specs,
        check_vma=False,
    )
```

```python
import functools

import jax
import jax.numpy as jnp
from jax import lax
from jax.experimental import pallas as pl
from jax.experimental.pallas import tpu as pltpu
from jax.sharding import PartitionSpec as P

MESH = pl.DeviceIdType.MESH
DB = 64
LANES = 128
HALF = DB // 2
WIDE_Y = 4
STRIDE = 2
TINY = 1e-30
NAMES = ("n", "c", "rr", "rf", "fg", "ri", "rg", "e")


def lane_low(rows):
    return lax.broadcasted_iota(jnp.int32, (rows, LANES), 1) < DB


def swap(x):
    return pltpu.roll(x, DB, 1)


def split(x):
    high = x.astype(jnp.bfloat16)
    low = (x - high.astype(jnp.float32)).astype(jnp.bfloat16)
    return high, low


def total(x):
    return jnp.sum(jnp.sum(x, axis=0, keepdims=True), axis=1, keepdims=True)


def recenter(stat, center):
    shift = stat["e"] - center
    return {
        "n": stat["n"],
        "c": stat["c"],
        "rr": stat["rr"] + 2.0 * shift * stat["rf"] + shift * shift * stat["n"],
        "rf": stat["rf"] + shift * stat["n"],
        "fg": stat["fg"] + shift * stat["c"],
        "ri": stat["ri"] + shift * stat["c"],
        "rg": stat["rg"] + shift * (stat["ri"] + stat["fg"]) + shift * shift * stat["c"],
    }


def quotient(cross, norm):
    return jnp.where(norm > TINY, cross / jnp.maximum(norm, TINY), 0.0)


def merge(stat, last):
    norm = jnp.sum(stat["n"], axis=0, keepdims=True)
    cross = jnp.sum(stat["c"], axis=0, keepdims=True)
    center = cross / norm if last else quotient(cross, norm)
    moved = recenter(stat, center)
    out = {name: jnp.sum(value, axis=0, keepdims=True) for name, value in moved.items()}
    out["e"] = center
    return out


def read_rows(buf):
    rows = buf[:, 0, :]
    return {name: rows[:, k : k + 1] for k, name in enumerate(NAMES)}


def row_of(stat):
    lane = lax.broadcasted_iota(jnp.int32, (1, LANES), 1)
    row = jnp.zeros((1, LANES), jnp.float32)
    for k, name in enumerate(NAMES):
        row = jnp.where(lane == k, stat[name], row)
    return row


def repack(src, dst):
    low = lane_low(src.shape[0])
    for u in range(HALF // 2):
        first = src[:, LANES * u : LANES * (u + 1)]
        second = src[:, LANES * (u + HALF // 2) : LANES * (u + HALF // 2 + 1)]
        dst[:, 2 * u, :] = jnp.where(low, first, swap(second))
        dst[:, 2 * u + 1, :] = jnp.where(low, swap(first), second)


def kernel(
    geo,
    wave_hbm,
    left_hbm,
    right_hbm,
    target_hbm,
    dims_hbm,
    out_ref,
    proj_ref,
    wave,
    left_ref,
    right_ref,
    target_ref,
    dims,
    asked,
    tab_vmem,
    tab,
    ready,
    other,
    shifts,
    zbuf,
    stage,
    rrecv,
    lall,
    lbf,
    wcat,
    rcat,
    gbuf,
    red_a,
    red_b,
    in_sem,
    out_sem,
    tab_sem,
    z_send,
    z_recv,
    p_send,
    p_recv,
    l_send,
    l_recv,
    a_send,
    a_recv,
    b_send,
    b_recv,
    g_send,
    g_pass,
    g_recv,
    plane_sem,
    space_sem,
):
    wide_x, wide_y, wide_z = geo
    terms = 2 * wide_x
    nblk = wide_z // 2
    half_z = wide_z // 2
    sec, pairs = wave.shape[0], wave.shape[2] // DB
    cells = sec * pairs
    chunks = z_send.shape[1]
    csec = sec // chunks
    plane = terms * wide_y

    my_t = lax.axis_index("terms")
    my_s = lax.axis_index("sectors")
    my_x = my_t // 2
    my_c = my_t % 2
    my_z = my_s // wide_y
    my_y = my_s % wide_y

    def dev(t, z, y):
        return {"terms": t, "sectors": z * wide_y + y}

    def plane_peer(i):
        other = lax.rem(my_t * wide_y + my_y + i, plane)
        return dev(other // wide_y, my_z, other % wide_y)

    def z_peer(i):
        return dev(my_t, lax.rem(my_z + i, wide_z), my_y)

    def y_peer(i):
        return dev(my_t, my_z, lax.rem(my_y + i, wide_y))

    def term_peer(i):
        return dev(lax.rem(my_t + i, terms), my_z, my_y)

    barrier = pltpu.get_barrier_semaphore()
    near = sorted({1, STRIDE, wide_z - STRIDE, wide_z - 1})

    def tell(sem, peers):
        for peer in peers:
            pl.semaphore_signal(sem, inc=1, device_id=peer, device_id_type=MESH)

    z_near = [z_peer(i) for i in near]
    y_near = [y_peer(i) for i in range(1, wide_y)]
    loads = [
        pltpu.make_async_copy(src, dst, in_sem.at[k])
        for k, (src, dst) in enumerate(
            (
                (right_hbm.at[0], right_ref),
                (left_hbm.at[0], left_ref),
                (target_hbm, target_ref),
                (dims_hbm, dims),
                (wave_hbm, wave),
            )
        )
    ]
    for load in loads:
        load.start()
    tell(barrier, z_near + y_near + [term_peer(i) for i in range(1, terms)])
    loads[0].wait()
    repack(right_ref, zbuf.at[0])
    pl.semaphore_wait(barrier, len(near) + wide_y - 1 + terms - 1)

    def z_copy(src, dst, k, peer):
        part = pl.ds(k * csec, csec)
        return pltpu.make_async_remote_copy(
            src_ref=zbuf.at[src, part],
            dst_ref=zbuf.at[dst, part],
            send_sem=z_send.at[dst, k],
            recv_sem=z_recv.at[dst, k],
            device_id=peer,
            device_id_type=MESH,
        )

    up, down = z_peer(STRIDE), z_peer(wide_z - STRIDE)

    def forward_up(o, k):
        z_copy(o, o + STRIDE, k, up).start()

    def forward_down(o, k):
        z_copy(o, (o + wide_z - STRIDE) % wide_z, k, down).start()

    sibling = dev(my_t + 1 - 2 * my_c, my_z, my_y)

    def l_copy(t, peer, k):
        return pltpu.make_async_remote_copy(
            src_ref=lall.at[t],
            dst_ref=lall.at[t],
            send_sem=l_send.at[k],
            recv_sem=l_recv.at[t],
            device_id=peer,
            device_id_type=MESH,
        )

    def x_term(i):
        return lax.rem(my_x + i, wide_x) * 2 + my_c

    for k in range(chunks):
        forward_up(0, k)
        forward_down(0, k)
    loads[1].wait()
    repack(left_ref, lall.at[my_t])
    for i in range(1, wide_x):
        l_copy(my_t, dev(x_term(i), my_z, my_y), i - 1).start()
    l_copy(my_t, sibling, wide_x - 1).start()

    tell(plane_sem, y_near)

    plan = piece_plan(geo)
    for k in range(2, 5):
        loads[k].wait()
    width = min(LANES, target_ref.shape[1])
    sec_bits, y_bits = sec.bit_length() - 1, wide_y.bit_length() - 1
    tile_lane = lax.broadcasted_iota(jnp.int32, (pairs, width), 1)
    tile_row = lax.broadcasted_iota(jnp.int32, (pairs, width), 0)

    def run_tile(run):
        base = lax.div(run * sec, width) * width
        tile = target_ref[:, pl.ds(pl.multiple_of(base, width), width)]
        return tile, ((tile_lane + base) >> sec_bits) == run

    def ask(o, step, first, last):
        far = (o + step) % wide_z
        wanted = lax.rem(my_z + (wide_z - o), wide_z) * wide_y + my_y

        def one(yp):
            reader = lax.rem(my_z + (wide_z + step), wide_z) * wide_y + yp
            tile, own = run_tile(reader)
            hit = jnp.logical_and(own, (tile >> sec_bits) == wanted)
            value = total(jnp.where(hit, (tile & (sec - 1)).astype(jnp.float32), 0.0))
            asked[far, yp] = jnp.broadcast_to(value, (8, LANES))

        for yp in range(first, last):
            one(yp)

    for pieces in plan:
        for one in pieces:
            ask(*one)
    tile, own = run_tile(my_s)
    run = tile >> sec_bits
    far = (my_z - (run >> y_bits) + wide_z) & (wide_z - 1)
    column = ((run & (wide_y - 1)) + my_y + far) & (wide_x - 1)
    slot = (2 * column + (far >> (half_z.bit_length() - 1))) * nblk + (far & (nblk - 1))
    tab_vmem[0:pairs, 0:width] = slot
    full_row = lax.broadcasted_iota(jnp.int32, (8, LANES), 0)
    full_lane = lax.broadcasted_iota(jnp.int32, (8, LANES), 1)
    found = jnp.zeros((8, LANES), jnp.float32)
    for b in range(nblk):
        hit = jnp.logical_and(own, slot == my_t * nblk + b)
        for k, what in enumerate((tile_lane & (sec - 1), tile_row, tile)):
            value = total(jnp.where(hit, what.astype(jnp.float32), 0.0))
            here = jnp.logical_and(full_row == b, full_lane == k)
            found = jnp.where(here, value, found)
    tab_vmem[8:16, :] = found.astype(jnp.int32)
    tab_copy = pltpu.make_async_copy(tab_vmem, tab, tab_sem)
    tab_copy.start()
    pl.semaphore_wait(plane_sem, wide_y - 1)
    tell(space_sem, z_near)

    def owner(far, step, yp):
        t = 2 * lax.rem(my_y + yp + far, wide_x) + far // half_z
        if step != 0:
            return t, jnp.bool_(False)
        return t, jnp.logical_and(t == my_t, yp == my_y)

    def remote_piece(far, step, yp):
        t, _ = owner(far, step, yp)
        return pltpu.make_async_remote_copy(
            src_ref=stage.at[far, yp],
            dst_ref=rrecv.at[far % half_z, my_t],
            send_sem=p_send.at[far, yp],
            recv_sem=p_recv.at[far % half_z],
            device_id=dev(t, lax.rem(my_z + (wide_z + step), wide_z), yp),
            device_id_type=MESH,
        )

    def local_piece(far, yp):
        b = far % half_z
        return pltpu.make_async_copy(stage.at[far, yp], rrecv.at[b, my_t], p_recv.at[b])

    def hand_out(o, step, first, last):
        far = (o + step) % wide_z

        def one(yp, carry):
            wanted = asked[far, yp]
            picks = [wanted == k for k in range(1, sec)]
            for r in range(0, HALF, 8):
                got = zbuf[o, 0, r : r + 8]
                for k in range(1, sec):
                    got = jnp.where(picks[k - 1], zbuf[o, k, r : r + 8], got)
                stage[far, yp, r : r + 8] = got
            if step != 0:
                remote_piece(far, step, yp).start()
                return carry
            _, mine = owner(far, step, yp)

            @pl.when(mine)
            def _():
                local_piece(far, yp).start()

            @pl.when(jnp.logical_not(mine))
            def _():
                remote_piece(far, step, yp).start()

            return carry

        lax.fori_loop(first, last, one, 0, unroll=True)

    def sent(o, step, first, last):
        far = (o + step) % wide_z

        def one(yp, carry):
            if step != 0:
                remote_piece(far, step, yp).wait_send()
                return carry
            _, mine = owner(far, step, yp)

            @pl.when(jnp.logical_not(mine))
            def _():
                remote_piece(far, step, yp).wait_send()

            return carry

        lax.fori_loop(first, last, one, 0)

    def arrive(o, k):
        z_copy(o, o, k, up).wait_recv()

    levels = len(plan) - 1

    def relay(n):
        for k in range(chunks):
            arrive(STRIDE * n, k)
            if n < levels:
                forward_up(STRIDE * n, k)
            arrive(wide_z - STRIDE * n, k)
            if n < levels:
                forward_down(wide_z - STRIDE * n, k)

    def pass_on(n):
        for one in sorted(plan[n], key=lambda piece: -abs(piece[1])):
            hand_out(*one)

    low64 = lane_low(DB)
    low32 = lane_low(HALF)
    lane = lax.broadcasted_iota(jnp.int32, (DB, LANES), 1)
    row = lax.broadcasted_iota(jnp.int32, (DB, LANES), 0)

    both_now = range(2)

    def apply(vecs, qs):
        rhs = []
        for k in both_now:
            vh, vl = split(vecs[k])
            rhs.append(jnp.concatenate([vh, vh, vl, vl], axis=0))
        for u in range(terms // 2):
            for k in both_now:
                lhs = lbf[qs[k], u * LANES : (u + 1) * LANES, :]
                part = jnp.dot(
                    jnp.concatenate([lhs, lhs], axis=1), rhs[k], preferred_element_type=jnp.float32
                )
                high, low = split(jnp.where(low64, part[:DB], part[DB:]))
                wcat[k, :DB, u * LANES : (u + 1) * LANES] = high
                wcat[k, DB:, u * LANES : (u + 1) * LANES] = low
        outs = []
        for k in both_now:
            out = lax.dot_general(
                wcat[k], rcat[k], (((1,), (1,)), ((), ())), preferred_element_type=jnp.float32
            )
            out = out[:DB] + out[DB:]
            outs.append(out + swap(out))
        return outs

    def pack(x):
        return jnp.where(low32, x[:HALF], x[HALF:])

    def work(m):
        low_b = jnp.where(my_c == 0, 2 * m, nblk - 2 - 2 * m)
        bs = [low_b, low_b + 1]
        for b in bs:
            pltpu.make_async_copy(rrecv.at[b], rrecv.at[b], p_recv.at[b]).wait()
        for k, b in enumerate(bs):
            for u in range(terms // 2):
                first, second = rrecv[b, 2 * u], rrecv[b, 2 * u + 1]
                top = jnp.where(low32, first, swap(second))
                bottom = jnp.where(low32, swap(first), second)
                high, low = split(jnp.concatenate([top, bottom], axis=0))
                rcat[k, :DB, u * LANES : (u + 1) * LANES] = high
                rcat[k, DB:, u * LANES : (u + 1) * LANES] = low
        qs, useds, firsts = [], [], []
        for b in bs:
            q, j = tab[8 + b, 0] & (sec - 1), tab[8 + b, 1]
            target = tab[8 + b, 2] & (dims.shape[0] - 1)
            column = jnp.full((DB, LANES), j >> 1, jnp.int32)
            odd = jnp.full((DB, LANES), j & 1, jnp.int32)
            raw = wave[q, :, 0:LANES]
            for u in range(1, pairs // 2):
                raw = jnp.where(column == u, wave[q, :, u * LANES : (u + 1) * LANES], raw)
            raw = jnp.where((lane >> 6) == odd, raw, swap(raw))
            used = jnp.logical_and(row < dims[my_s * sec + q], (lane & (DB - 1)) < dims[target])
            qs.append(q)
            useds.append(used)
            firsts.append(jnp.where(used, raw, 0.0))
        images = [jnp.where(useds[k], x, 0.0) for k, x in enumerate(apply(firsts, qs))]
        norms = [0.5 * total(firsts[k] * firsts[k]) for k in both_now]
        crosses = [0.5 * total(firsts[k] * images[k]) for k in both_now]
        energies = [quotient(crosses[k], norms[k]) for k in both_now]
        rests = [images[k] - energies[k] * firsts[k] for k in both_now]
        seconds = [jnp.where(useds[k], x, 0.0) for k, x in enumerate(apply(rests, qs))]
        sub = lax.broadcasted_iota(jnp.int32, (8, LANES), 0)
        for k, b in enumerate(bs):
            first, image, rest, second = firsts[k], images[k], rests[k], seconds[k]
            gbuf[my_t, b, :HALF] = pack(second)
            gbuf[my_t, b, HALF:DB] = pack(image)
            values = (
                norms[k],
                crosses[k],
                0.5 * total(rest * rest),
                0.5 * total(rest * first),
                0.5 * total(first * second),
                0.5 * total(rest * image),
                0.5 * total(rest * second),
                energies[k],
            )
            tile = jnp.zeros((8, LANES), jnp.float32)
            for n, value in enumerate(values):
                tile = jnp.where(sub == n, value, tile)
            gbuf[my_t, b, DB:] = tile
        return low_b

    def send_pair(low_b):
        for i in far_first(wide_x):
            g_pair(low_b, i - 1, dev(x_term(i), my_z, my_y)).start()
        g_pair(low_b, wide_x - 1, sibling).start()

    def g_pair(b, k, peer):
        return pltpu.make_async_remote_copy(
            src_ref=gbuf.at[my_t, pl.ds(b, 2)],
            dst_ref=gbuf.at[my_t, pl.ds(b, 2)],
            send_sem=g_send.at[b // 2, k],
            recv_sem=g_recv.at[my_t, b // 2],
            device_id=peer,
            device_id_type=MESH,
        )

    def g_copy(t, b, k, peer):
        return pltpu.make_async_remote_copy(
            src_ref=gbuf.at[t, pl.ds(b, 2)],
            dst_ref=gbuf.at[t, pl.ds(b, 2)],
            send_sem=g_pass.at[b // 2, k],
            recv_sem=g_recv.at[t, b // 2],
            device_id=peer,
            device_id_type=MESH,
        )

    def pass_pair(m):
        low_b = jnp.where(my_c == 0, 2 * m, nblk - 2 - 2 * m)
        for i in range(1, wide_x):
            g_copy(x_term(i), low_b, i - 1, sibling).wait_recv()
            g_copy(x_term(i), low_b, i - 1, sibling).start()

    def unpack_left():
        def one(t, carry):
            for q in range(sec):
                x = lall[t, q]
                high, low = split(x)
                high, low = high.astype(jnp.float32), low.astype(jnp.float32)
                top = jnp.where(low32, high, swap(low))
                bottom = jnp.where(low32, swap(high), low)
                both = jnp.concatenate([top, bottom], axis=0).astype(jnp.bfloat16)
                lbf[q, pl.ds(pl.multiple_of(t * DB, DB), DB), :] = both
            return carry

        lax.fori_loop(0, terms, one, 0)

    for n in range(1, levels + 1):
        relay(n)
        if n == 1:
            pl.semaphore_wait(space_sem, len(near))
            pass_on(0)
        pass_on(n)
        if n == min(2, levels):
            for i in range(1, wide_x):
                t = x_term(i)
                l_copy(t, sibling, 0).wait_recv()
                l_copy(t, sibling, wide_x - 1 + i).start()
    tab_copy.wait()
    for i in range(wide_x):
        l_copy(lax.rem(my_x + i, wide_x) * 2 + 1 - my_c, sibling, 0).wait_recv()
    unpack_left()
    for m in range(nblk // 2 - 1):
        send_pair(work(m))
    last_pair = work(nblk // 2 - 1)

    stat = {name: gbuf[my_t, :, DB + k, :] for k, name in enumerate(NAMES)}
    mine = my_t * wide_y + my_y
    red_b[my_z] = row_of(merge(stat, False))

    def a_copy(i):
        return pltpu.make_async_remote_copy(
            src_ref=red_a.at[mine],
            dst_ref=red_a.at[mine],
            send_sem=a_send.at[i],
            recv_sem=a_recv,
            device_id=plane_peer(i),
            device_id_type=MESH,
        )

    def b_copy(i):
        return pltpu.make_async_remote_copy(
            src_ref=red_b.at[my_z],
            dst_ref=red_b.at[my_z],
            send_sem=b_send.at[i],
            recv_sem=b_recv,
            device_id=z_peer(i),
            device_id_type=MESH,
        )

    for i in far_first(wide_z):
        b_copy(i).start()
    send_pair(last_pair)
    for m in range(nblk // 2 - 1):
        pass_pair(m)
    pltpu.make_async_copy(
        red_b.at[pl.ds(0, wide_z - 1)], red_b.at[pl.ds(0, wide_z - 1)], b_recv
    ).wait()
    red_a[mine] = row_of(merge(read_rows(red_b), False))
    lax.fori_loop(1, plane, lambda i, c: (a_copy(i).start(), c)[1], 0)
    pass_pair(nblk // 2 - 1)
    for m in range(nblk // 2):
        for i in range(wide_x):
            g_copy(lax.rem(my_x + i, wide_x) * 2 + 1 - my_c, 2 * m, 0, sibling).wait_recv()

    def place(q, carry):
        for u in range(pairs // 2):
            ats = [tab[2 * u + k, lax.rem(my_s * sec, width) + q] for k in range(2)]
            parts = [(at // nblk, lax.rem(at, nblk)) for at in ats]
            for dst, lo in ((ready, 0), (other, HALF)):
                first, second = [gbuf[t, b, lo : lo + HALF] for t, b in parts]
                dst[q, 0:HALF, u * LANES : (u + 1) * LANES] = jnp.where(
                    low32, first, swap(second)
                )
                dst[q, HALF:DB, u * LANES : (u + 1) * LANES] = jnp.where(
                    low32, swap(first), second
                )
            first, second = [gbuf[t, b, DB : DB + 8] for t, b in parts]
            shifts[q, :, u * LANES : (u + 1) * LANES] = jnp.where(low32[:8], first, second)
        return carry

    lax.fori_loop(0, sec, place, 0)

    for n in range(len(plan) - 1):
        for k in range(chunks):
            z_copy(0, STRIDE * (n + 1), k, up).wait_send()
            z_copy(0, wide_z - STRIDE * (n + 1), k, down).wait_send()
    for pieces in plan:
        for one in pieces:
            sent(*one)
    for i in range(2 * wide_x - 1):
        l_copy(my_t, sibling, i).wait_send()

    def g_done(b, carry):
        for k in range(wide_x):
            g_pair(2 * b, k, sibling).wait_send()
        return carry

    lax.fori_loop(0, nblk // 2, g_done, 0)
    for m in range(nblk // 2):
        for i in range(wide_x - 1):
            g_copy(my_t, 2 * m, i, sibling).wait_send()
    lax.fori_loop(1, wide_z, lambda i, c: (b_copy(i).wait_send(), c)[1], 0)
    pltpu.make_async_copy(
        red_a.at[pl.ds(0, plane - 1)], red_a.at[pl.ds(0, plane - 1)], a_recv
    ).wait()
    final = merge(read_rows(red_a), True)
    cell_total = float(plane * wide_z * nblk * DB * DB)
    squared = jnp.maximum(final["rr"], 0.0)
    scale = 1.0 / jnp.sqrt(squared / cell_total + 1e-06)
    sub2 = lax.broadcasted_iota(jnp.int32, (2, 2), 0)
    lane2 = lax.broadcasted_iota(jnp.int32, (2, 2), 1)
    proj_ref[...] = (
        jnp.where(
            sub2 == 0,
            jnp.where(lane2 == 0, final["c"], final["fg"] * scale),
            jnp.where(lane2 == 0, final["ri"] * scale, final["rg"] * scale * scale),
        )
        / cell_total
    )

    for q in range(sec):
        shift = shifts[q, 7:8, :] - final["e"][:, :1]
        ready[q] = (ready[q] + shift * other[q]) * scale
        pltpu.make_async_copy(ready.at[q], out_ref.at[q], out_sem.at[q]).start()
    lax.fori_loop(1, plane, lambda i, c: (a_copy(i).wait_send(), c)[1], 0)
    for q in range(sec):
        pltpu.make_async_copy(ready.at[q], out_ref.at[q], out_sem.at[q]).wait()


def far_first(count):
    return sorted(range(1, count), key=lambda i: -min(i, count - i))


def piece_plan(geo):
    _, wide_y, wide_z = geo
    levels = wide_z // (2 * STRIDE)
    plan = []
    for n in range(levels):
        o = STRIDE * n
        pieces = []
        for step in range(STRIDE):
            pieces.append((o, step, 0, wide_y))
            if o + step > 0:
                pieces.append(((wide_z - o) % wide_z, -step, 0, wide_y))
        plan.append(pieces)
    top = STRIDE * (levels - 1)
    plan[-1].append((top, STRIDE, 0, wide_y // 2))
    plan[-1].append(((wide_z - top) % wide_z, -STRIDE, wide_y // 2, wide_y))
    return plan


def per_device(wide_y, wave, left_env, right_env, pair_target, block_dims):
    terms = lax.axis_size("terms")
    devices = lax.axis_size("sectors")
    geo = (terms // 2, wide_y, devices // wide_y)
    sec = wave.shape[0]
    pairs = wave.shape[2] // DB
    nblk = geo[2] // 2
    plane = terms * wide_y
    chunks = 4
    f32, bf16 = jnp.float32, jnp.bfloat16
    dma = pltpu.SemaphoreType.DMA
    vmem = pl.BlockSpec(memory_space=pltpu.VMEM)
    hbm = pl.BlockSpec(memory_space=pl.ANY)
    return pl.pallas_call(
        functools.partial(kernel, geo),
        out_shape=(
            jax.ShapeDtypeStruct(wave.shape, f32),
            jax.ShapeDtypeStruct((2, 2), f32),
        ),
        in_specs=[hbm] * 5,
        out_specs=(hbm, vmem),
        scratch_shapes=[
            pltpu.VMEM(wave.shape, f32),
            pltpu.VMEM((sec, DB * DB), f32),
            pltpu.VMEM((sec, DB * DB), f32),
            pltpu.VMEM((pairs, pair_target.shape[0]), jnp.int32),
            pltpu.SMEM(block_dims.shape, jnp.int32),
            pltpu.VMEM((geo[2], wide_y, 8, LANES), f32),
            pltpu.VMEM((16, LANES), jnp.int32),
            pltpu.SMEM((16, LANES), jnp.int32),
            pltpu.VMEM(wave.shape, f32),
            pltpu.VMEM(wave.shape, f32),
            pltpu.VMEM((sec, 8, pairs * DB), f32),
            pltpu.VMEM((geo[2], sec, HALF, LANES), f32),
            pltpu.VMEM((geo[2], wide_y, HALF, LANES), f32),
            pltpu.VMEM((nblk, terms, HALF, LANES), f32),
            pltpu.VMEM((terms, sec, HALF, LANES), f32),
            pltpu.VMEM((sec, terms * DB, LANES), bf16),
            pltpu.VMEM((2, LANES, terms * DB), bf16),
            pltpu.VMEM((2, LANES, terms * DB), bf16),
            pltpu.VMEM((terms, nblk, DB + 8, LANES), f32),
            pltpu.VMEM((plane, 1, LANES), f32),
            pltpu.VMEM((geo[2], 1, LANES), f32),
            dma((5,)),
            dma((sec,)),
            dma,
            dma((geo[2], chunks)),
            dma((geo[2], chunks)),
            dma((geo[2], wide_y)),
            dma((nblk,)),
            dma((2 * geo[0] - 1,)),
            dma((terms,)),
            dma((plane,)),
            dma,
            dma((geo[2],)),
            dma,
            dma((nblk // 2, geo[0])),
            dma((nblk // 2, geo[0])),
            dma((terms, nblk // 2)),
            pltpu.SemaphoreType.REGULAR,
            pltpu.SemaphoreType.REGULAR,
        ],
        compiler_params=pltpu.CompilerParams(
            collective_id=0, has_side_effects=True, vmem_limit_bytes=56 * 1024 * 1024
        ),
    )(
        wave,
        left_env,
        right_env,
        pair_target.T,
        block_dims,
    )


def solution(mesh, wide_y=WIDE_Y):
    in_specs = (
        P("sectors", None, None),
        P("terms", "sectors", None),
        P("terms", "sectors", None),
        P(),
        P(),
    )
    out_specs = (P("sectors", None, None), P())
    return jax.shard_map(
        functools.partial(per_device, wide_y),
        mesh=mesh,
        in_specs=in_specs,
        out_specs=out_specs,
        check_vma=False,
    )
```
